32 devices in a mesh: tm: 16 (over z, y, x), rows: 2 (over core).
Axes of the slice: x: 2, y: 2, z: 4, core: 2. Of those that a mesh axis runs over, the one named last changes fastest.
Arguments:
- snapshots: bfloat16 [128, 32, 2048], P('tm', 'rows'), may hold values from -8 to 8
- tile_masks: int32 [128, 4, 16], P('tm', 'rows'), may hold values from 0 to 1, as said below
- widths: int32 [128, 2], P('tm'), may hold values from 1 to 4
Outputs:
- excess_map: float32 [2, 32, 2048], P(None, 'rows', 'tm')
- peak_map: float32 [2, 32, 2048], P(None, 'rows')
The draws below stay inside these ranges and needn't reach their ends.
Inputs may be any that keep to these rules, and one draw needn't show every extreme that they name: `tile_masks`: 1 keeps the 8 x 128 tile of a snapshot, 0 rejects it.
All inputs are finite; a program needn't handle non-finite values.
Results may differ from the reference program's by a relative error of at most 0.0036.
Values may be sent and summed in bfloat16 or wider, within the bound.
A program may use at most 64 MiB of HBM per device.

```python
import jax
import jax.numpy as jnp
from jax import lax

COLS = 2048
T_DEV = 8
HISTORY_FRAMES = 64
RADIUS = 8
TILE_R = 8
TILE_C = 128
NFILT = 2
SNAPSHOT_TOTAL = 128
ROWS = 32


def draw_snapshots(key, part):
    sky_key = jax.random.fold_in(key, 11)
    noise_key = jax.random.fold_in(key, 12)
    sky_level = 1.5 * jax.random.normal(sky_key, (ROWS, COLS), jnp.float32)
    noise_part = jax.random.normal(noise_key, (SNAPSHOT_TOTAL, ROWS, COLS), jnp.float32)
    return jnp.clip(sky_level[None] + noise_part, -8.0, 8.0).astype(jnp.bfloat16)


def draw_tile_masks(key, part):
    patch_rows = ROWS // TILE_R
    patch_columns = COLS // TILE_C
    random_retain_mask = jax.random.randint(jax.random.fold_in(key, 21), (SNAPSHOT_TOTAL, patch_rows, patch_columns), 0, 10) >= 2
    contains_flare = jax.random.randint(jax.random.fold_in(key, 22), (patch_rows, patch_columns), 0, 8) == 0
    flare_onset = jax.random.randint(jax.random.fold_in(key, 23), (patch_rows, patch_columns), 0, SNAPSHOT_TOTAL)
    flare_length = jax.random.randint(jax.random.fold_in(key, 24), (patch_rows, patch_columns), HISTORY_FRAMES + 1, 3 * HISTORY_FRAMES)
    snapshot_index = jnp.arange(SNAPSHOT_TOTAL)[:, None, None]
    inside_flare = contains_flare[None] & (snapshot_index >= flare_onset[None]) & (snapshot_index < flare_onset[None] + flare_length[None])
    return jnp.where(inside_flare | jnp.logical_not(random_retain_mask), 0, 1).astype(jnp.int32)


def plant(array, own_key, low, largest):
    spot = [jax.random.randint(jax.random.fold_in(own_key, axis), (), 0, length) for axis, length in enumerate(array.shape)]
    main_axis = array.shape.index(max(array.shape))
    next_to = spot[:main_axis] + [(spot[main_axis] + 1) % array.shape[main_axis]] + spot[main_axis + 1:]
    return array.at[tuple(spot)].set(low).at[tuple(next_to)].set(largest)


def setup_inputs(seed: int = 0) -> dict:
    arg_keys = jax.random.split(jax.random.key(seed), 4)
    return {
        "snapshots": draw_snapshots(jax.random.fold_in(arg_keys[3], 71), 0),
        "tile_masks": draw_tile_masks(jax.random.fold_in(arg_keys[3], 71), 0),
        "widths": plant(jax.random.randint(arg_keys[2], (SNAPSHOT_TOTAL, NFILT), 1, 5), jax.random.fold_in(arg_keys[2], 1), 1, 4).astype(jnp.int32),
    }


threshold = 0.5

def expand_tiles(tile_values):
    frame_count, patch_rows, patch_columns = tile_values.shape
    spread = jnp.broadcast_to(tile_values[:, :, None, :, None], (frame_count, patch_rows, TILE_R, patch_columns, TILE_C))
    return spread.reshape(frame_count, patch_rows * TILE_R, patch_columns * TILE_C)

def filter_taps(widths):
    sigma_val = widths.astype(jnp.float32)[..., None]
    offsets = jnp.arange(-RADIUS, RADIUS + 1).astype(jnp.float32)
    weights = jnp.exp(-(offsets * offsets) / (2.0 * sigma_val * sigma_val))
    return (weights / jnp.sqrt(lax.optimization_barrier(jnp.sum(weights * weights, axis=-1, keepdims=True)))).astype(jnp.bfloat16)

def reference(snapshots, tile_masks, widths):
    padded_frames = jnp.concatenate([jnp.zeros((HISTORY_FRAMES, ROWS, COLS), jnp.bfloat16), snapshots], axis=0)
    padded_masks = jnp.concatenate([jnp.zeros((HISTORY_FRAMES,) + tile_masks.shape[1:], jnp.int32), tile_masks], axis=0)
    window_rows = jnp.arange(T_DEV)[:, None]
    window_cols = jnp.arange(HISTORY_FRAMES + T_DEV)[None, :]
    window_band = ((window_cols >= window_rows) & (window_cols < window_rows + HISTORY_FRAMES)).astype(jnp.float32)

    def block_step(totals, block_index):
        excess_sum, peak_now = totals
        first_time = (block_index * T_DEV).astype(jnp.int32)
        history = lax.dynamic_slice_in_dim(padded_frames, first_time, HISTORY_FRAMES + T_DEV, 0).astype(jnp.float32)
        history_masks = lax.dynamic_slice_in_dim(padded_masks, first_time, HISTORY_FRAMES + T_DEV, 0).astype(jnp.float32)
        masked_hist = history * expand_tiles(history_masks)
        window = jnp.einsum('js,src->jrc', window_band, masked_hist, precision=lax.Precision.HIGHEST)
        counts = jnp.einsum('js,src->jrc', window_band, history_masks, precision=lax.Precision.HIGHEST)
        current = lax.dynamic_slice_in_dim(snapshots, first_time, T_DEV, 0).astype(jnp.float32)
        current_keep = expand_tiles(lax.dynamic_slice_in_dim(tile_masks, first_time, T_DEV, 0).astype(jnp.float32))
        mean_img = window / expand_tiles(jnp.maximum(counts, 1.0))
        residual = (current_keep * (current - mean_img)).astype(jnp.bfloat16)
        kernel = filter_taps(lax.dynamic_slice_in_dim(widths, first_time, T_DEV, 0)).astype(jnp.float32)
        row_padded = jnp.pad(residual.astype(jnp.float32), ((0, 0), (RADIUS, RADIUS), (0, 0)))
        excess_list = []
        peak_list = []
        for filter_index in range(NFILT):
            summed = jnp.zeros((T_DEV, ROWS, COLS), jnp.float32)
            for offset in range(2 * RADIUS + 1):
                summed = summed + kernel[:, filter_index, offset][:, None, None] * row_padded[:, offset:offset + ROWS, :]
            row_out = summed.astype(jnp.bfloat16)
            column_padded = jnp.pad(row_out.astype(jnp.float32), ((0, 0), (0, 0), (RADIUS, RADIUS)))
            filtered = jnp.zeros((T_DEV, ROWS, COLS), jnp.float32)
            for offset in range(2 * RADIUS + 1):
                filtered = filtered + kernel[:, filter_index, offset][:, None, None] * column_padded[:, :, offset:offset + COLS]
            excess_list.append(lax.optimization_barrier(jnp.sum(jnp.maximum(filtered - threshold, 0.0), axis=0)))
            peak_list.append(lax.optimization_barrier(jnp.max(filtered, axis=0)))
        excess_sum = excess_sum + jnp.stack(excess_list)
        peak_now = jnp.maximum(peak_now, jnp.stack(peak_list))
        return ((excess_sum, peak_now), None)
    initial = (jnp.zeros((NFILT, ROWS, COLS), jnp.float32), jnp.full((NFILT, ROWS, COLS), -1e+30, jnp.float32))
    (excess_sum, peak_map), unused = lax.scan(block_step, initial, jnp.arange(SNAPSHOT_TOTAL // T_DEV, dtype=jnp.int32))
    return (excess_sum / SNAPSHOT_TOTAL, peak_map)
```

```python
import functools
import math

import jax
import jax.numpy as jnp
from jax import lax
from jax.experimental import pallas as pl
from jax.experimental.pallas import tpu as pltpu
from jax.sharding import PartitionSpec as P

HISTORY_FRAMES = 64
RADIUS = 8
TILE_R = 8
TILE_C = 128


threshold = 0.5


def padded(value, sides, width):
    for axis, dim in sides:
        count, length = (lax.axis_size(axis), value.shape[dim])
        up = [(i, (i + 1) % count) for i in range(count - 1)]
        down = [(j, i) for i, j in up]
        last = lax.slice_in_dim(value, length - width, length, axis=dim)
        first = lax.slice_in_dim(value, 0, width, axis=dim)
        before = lax.ppermute(last, axis, up)
        after = lax.ppermute(first, axis, down)
        value = jnp.concatenate([before, value, after], axis=dim)
    return value


def filter_taps(widths):
    sigma_val = widths.astype(jnp.float32)[..., None]
    offsets = jnp.arange(-RADIUS, RADIUS + 1).astype(jnp.float32)
    weights = jnp.exp(-(offsets * offsets) / (2.0 * sigma_val * sigma_val))
    return (weights / jnp.sqrt(jnp.sum(weights * weights, axis=-1, keepdims=True))).astype(
        jnp.bfloat16
    )


def history_band(local_times, back_step):
    target = jnp.arange(local_times)[:, None]
    source = jnp.arange(local_times)[None, :]
    distance = back_step * local_times + target - source
    return ((distance >= 1) & (distance <= HISTORY_FRAMES)).astype(jnp.bfloat16)


def tap_onehot(target_count):
    taps_count = 2 * RADIUS + 1
    source = jnp.arange(target_count + 2 * RADIUS)[:, None, None]
    target = jnp.arange(target_count)[None, :, None]
    return (source - target == jnp.arange(taps_count)[None, None, :]).astype(jnp.float32)


def column_residual(snapshots, tile_masks, widths):
    moved = lax.all_to_all(snapshots, "tm", split_axis=2, concat_axis=0, tiled=True)
    all_masks, all_widths = (
        lax.all_gather(tile_masks, "tm", axis=0, tiled=True),
        lax.all_gather(widths, "tm", axis=0, tiled=True),
    )
    total_times, local_rows, own_cols = moved.shape
    patch_rows = all_masks.shape[1]
    first_col = lax.axis_index("tm") * own_cols
    tile_of = (first_col + jnp.arange(own_cols)) // TILE_C
    pick = (jnp.arange(all_masks.shape[2])[:, None] == tile_of[None, :]).astype(jnp.float32)
    keep_tiles = jnp.einsum("trk,kc->trc", all_masks.astype(jnp.float32), pick)
    keep_pixels = jnp.broadcast_to(
        keep_tiles[:, :, None, :], (total_times, patch_rows, TILE_R, own_cols)
    ).reshape(total_times, local_rows, own_cols)
    pixels = local_rows * own_cols
    keep_flat = keep_pixels.astype(jnp.bfloat16).reshape(total_times, pixels)
    masked = moved.reshape(total_times, pixels) * keep_flat
    block_count = total_times // HISTORY_FRAMES
    own_band = history_band(HISTORY_FRAMES, 0)
    back_band = history_band(HISTORY_FRAMES, 1)
    empty_block = jnp.zeros((1, HISTORY_FRAMES, pixels), jnp.bfloat16)
    value_blocks = masked.reshape(block_count, HISTORY_FRAMES, pixels)
    keep_blocks = keep_flat.reshape(block_count, HISTORY_FRAMES, pixels)
    value_prior = jnp.concatenate([empty_block, value_blocks[:-1]], axis=0)
    keep_prior = jnp.concatenate([empty_block, keep_blocks[:-1]], axis=0)
    window = jnp.einsum("js,bsp->bjp", own_band, value_blocks, preferred_element_type=jnp.float32)
    window = window + jnp.einsum(
        "js,bsp->bjp", back_band, value_prior, preferred_element_type=jnp.float32
    )
    counts = jnp.einsum("js,bsp->bjp", own_band, keep_blocks, preferred_element_type=jnp.float32)
    counts = counts + jnp.einsum(
        "js,bsp->bjp", back_band, keep_prior, preferred_element_type=jnp.float32
    )
    mean_img = (window / jnp.maximum(counts, 1.0)).reshape(total_times, local_rows, own_cols)
    residual = (keep_pixels * (moved.astype(jnp.float32) - mean_img)).astype(jnp.bfloat16)
    return (residual, filter_taps(all_widths).astype(jnp.float32))


def body(snapshots, tile_masks, widths):
    residual, kernel = column_residual(snapshots, tile_masks, widths)
    local_times, local_rows, column_count = residual.shape
    padded_rows = padded(residual, (("rows", 1),), RADIUS)
    row_onehot = tap_onehot(local_rows)
    row_results = []
    for filter_index in range(widths.shape[1]):
        row_weights = jnp.einsum(
            "jik,tk->tij", row_onehot, kernel[:, filter_index], precision=lax.Precision.HIGHEST
        ).astype(jnp.bfloat16)
        row_results.append(
            jnp.einsum(
                "tij,tjc->tic", row_weights, padded_rows, preferred_element_type=jnp.float32
            ).astype(jnp.bfloat16)
        )
    stacked_rows = jnp.stack(row_results)
    padded_cols = padded(stacked_rows, (("tm", 3),), RADIUS)
    column_onehot = tap_onehot(column_count)
    excess_terms = []
    peak_terms = []
    for filter_index in range(widths.shape[1]):
        column_weights = jnp.einsum(
            "jck,tk->tjc", column_onehot, kernel[:, filter_index], precision=lax.Precision.HIGHEST
        ).astype(jnp.bfloat16)
        filtered = jnp.einsum(
            "trj,tjc->trc",
            padded_cols[filter_index],
            column_weights,
            preferred_element_type=jnp.float32,
        )
        excess_terms.append(jnp.sum(jnp.maximum(filtered - threshold, 0.0), axis=0))
        peak_terms.append(jnp.max(filtered, axis=0))
    excess_map = jnp.stack(excess_terms) / local_times
    peak_map = lax.all_gather(jnp.stack(peak_terms), "tm", axis=2, tiled=True)
    return (excess_map, peak_map)


MESH = pl.DeviceIdType.MESH
WIDTHS = 4
LANES = 128
HALO_ROWS = 8


def tap_values(offset, width):
    norm = math.sqrt(sum(math.exp(-(k * k) / (width * width)) for k in range(-RADIUS, RADIUS + 1)))
    value = jnp.exp(offset * offset * (-1.0 / (2.0 * width * width))) / norm
    return jnp.where(jnp.abs(offset) <= RADIUS, value, 0.0)


def pick_width(width, options):
    first, second, third, fourth = options
    return jnp.where(
        width == 1.0,
        first,
        jnp.where(width == 2.0, second, jnp.where(width == 3.0, third, fourth)),
    )


def search_kernel(
    n,
    x_ref,
    meta_ref,
    exc_ref,
    peak_ref,
    x_all,
    halo_out,
    halo_all,
    meta_all,
    keep_rows,
    scale_rows,
    width_rows,
    masked,
    resid,
    resid_out,
    row_w,
    row_tab,
    col_tab,
    spread,
    peak_out,
    peak_all,
    x_send,
    x_recv,
    meta_send,
    meta_recv,
    halo_send,
    halo_recv,
    row_send,
    row_recv,
    peak_send,
    peak_recv,
):
    me, core = lax.axis_index("tm"), lax.axis_index("rows")
    td = x_ref.shape[0]
    rows = x_ref.shape[1]
    total = n * td
    f32, bf16 = jnp.float32, jnp.bfloat16

    def peer(step):
        return lax.rem(me + step, n)

    def lanes_of(band):
        return pl.ds(pl.multiple_of(band * LANES, LANES), LANES)

    def x_copy(source, target):
        return pltpu.make_async_remote_copy(
            src_ref=x_ref.at[:, :, lanes_of(target)],
            dst_ref=x_all.at[source],
            send_sem=x_send.at[target],
            recv_sem=x_recv.at[source],
            device_id={"tm": target},
            device_id_type=MESH,
        )

    def meta_copy(source, target):
        return pltpu.make_async_remote_copy(
            src_ref=meta_ref,
            dst_ref=meta_all.at[source],
            send_sem=meta_send.at[target],
            recv_sem=meta_recv.at[source],
            device_id={"tm": target},
            device_id_type=MESH,
        )

    def halo_copy(source, target):
        return pltpu.make_async_remote_copy(
            src_ref=halo_out.at[target],
            dst_ref=halo_all.at[source],
            send_sem=halo_send.at[target],
            recv_sem=halo_recv.at[source],
            device_id={"tm": target},
            device_id_type=MESH,
        )

    def row_copy(chunk):
        return pltpu.make_async_remote_copy(
            src_ref=resid_out.at[chunk],
            dst_ref=resid.at[chunk, pl.ds(td * rows, td * HALO_ROWS)],
            send_sem=row_send.at[chunk],
            recv_sem=row_recv.at[chunk],
            device_id={"rows": 1 - core},
            device_id_type=MESH,
        )

    def peak_copy(source, target):
        return pltpu.make_async_remote_copy(
            src_ref=peak_out,
            dst_ref=peak_all.at[source],
            send_sem=peak_send.at[target],
            recv_sem=peak_recv.at[source],
            device_id={"tm": target},
            device_id_type=MESH,
        )

    barrier = pltpu.get_barrier_semaphore()

    def greet(step, carry):
        pl.semaphore_signal(barrier, inc=1, device_id={"tm": peer(step)}, device_id_type=MESH)
        return carry

    lax.fori_loop(1, n, greet, 0)
    pl.semaphore_signal(barrier, inc=1, device_id={"rows": 1 - core}, device_id_type=MESH)
    pl.semaphore_wait(barrier, n)

    def send_first(step, carry):
        meta_copy(me, peer(step)).start()
        x_copy(me, peer(step)).start()
        return carry

    lax.fori_loop(1, n, send_first, 0)

    side = 2 * RADIUS
    lane_in = lax.broadcasted_iota(jnp.int32, (LANES, 2 * LANES), 0)
    lane_out = lax.broadcasted_iota(jnp.int32, (LANES, 2 * LANES), 1)
    packed = jnp.zeros((n * rows, 2 * LANES), f32)
    for j in range(td):
        tiles = jnp.concatenate(
            [x_ref[j, :, d * LANES : (d + 1) * LANES] for d in range(n)], axis=0
        )
        to_right = (lane_in >= LANES - RADIUS) & (
            lane_out == lane_in - (LANES - RADIUS) + side * j
        )
        to_left = (lane_in < RADIUS) & (lane_out == LANES + lane_in + RADIUS + side * j)
        packed = packed + jnp.dot(
            tiles, (to_right | to_left).astype(f32).astype(bf16), preferred_element_type=f32
        )
    for d in range(n):
        tile = jnp.zeros((rows, LANES), f32)
        if d > 0:
            tile = tile + packed[(d - 1) * rows : d * rows, :LANES]
        if d < n - 1:
            tile = tile + packed[(d + 1) * rows : (d + 2) * rows, LANES:]
        halo_out[d] = tile.astype(bf16)

    def send_halo(step, carry):
        halo_copy(me, peer(step)).start()
        return carry

    lax.fori_loop(1, n, send_halo, 0)
    meta_all[me] = meta_ref[...]
    halo_all[me] = halo_out[me]
    x_all[me] = x_ref[:, :, lanes_of(me)]

    spread_in = lax.broadcasted_iota(jnp.int32, spread.shape, 0)
    spread_out = lax.broadcasted_iota(jnp.int32, spread.shape, 1)
    spread[...] = (
        (spread_out % LANES < side) & (spread_in == side * (spread_out // LANES) + spread_out % LANES)
    ).astype(f32).astype(bf16)
    lane = lax.broadcasted_iota(jnp.int32, (2 * LANES, LANES), 0)
    column = lax.broadcasted_iota(jnp.int32, (2 * LANES, LANES), 1)
    source_col = jnp.where(
        lane < LANES,
        lane,
        jnp.where(
            lane < LANES + RADIUS,
            lane - LANES - RADIUS,
            jnp.where(lane < LANES + side, lane - RADIUS, 4 * LANES),
        ),
    )
    column_offset = (source_col - column).astype(f32)
    for s in range(WIDTHS):
        col_tab[:, s * LANES : (s + 1) * LANES] = tap_values(column_offset, s + 1).astype(bf16)
    out_row = lax.broadcasted_iota(jnp.int32, (rows, 2 * LANES), 0)
    lane = lax.broadcasted_iota(jnp.int32, (rows, 2 * LANES), 1)
    own = lane < td * rows
    beside = lane - td * rows
    time_of = jnp.where(own, lane // rows, beside // HALO_ROWS)
    source_row = jnp.where(own, lane % rows, beside % HALO_ROWS + jnp.where(core == 0, rows, -HALO_ROWS))
    row_offset = (source_row - out_row).astype(f32)
    for s in range(WIDTHS):
        values = tap_values(row_offset, s + 1).astype(bf16).astype(f32)
        for j in range(td):
            row_tab[s, j] = jnp.where(time_of == j, values, 0.0)
    masked[0:HISTORY_FRAMES] = jnp.zeros((HISTORY_FRAMES,) + masked.shape[1:], f32)

    def wait_meta(step, carry):
        meta_copy(peer(step), me).wait_recv()
        return carry

    lax.fori_loop(1, n, wait_meta, 0)
    meta = meta_all[...].reshape(total, LANES).astype(bf16)
    entry = lax.broadcasted_iota(jnp.int32, (LANES, 2 * LANES), 0)
    lane = lax.broadcasted_iota(jnp.int32, (LANES, 2 * LANES), 1)
    tile_of = jnp.where(
        lane < LANES,
        me,
        jnp.where(lane < LANES + RADIUS, me - 1, jnp.where(lane < LANES + side, me + 1, -1)),
    )
    inside = (tile_of >= 0) & (tile_of < n)
    target = lax.broadcasted_iota(jnp.int32, (total, total), 0)
    source = lax.broadcasted_iota(jnp.int32, (total, total), 1)
    band = ((target - source >= 1) & (target - source <= HISTORY_FRAMES)).astype(f32).astype(bf16)
    for rt in range(2):
        pick = (inside & (entry == rt * n + tile_of)).astype(f32).astype(bf16)
        keep = jnp.dot(meta, pick, preferred_element_type=f32)
        counts = jnp.dot(band, keep.astype(bf16), preferred_element_type=f32)
        keep_rows[rt] = keep
        scale_rows[rt] = keep / jnp.maximum(counts, 1.0)
    for f in range(2):
        pick = (entry == 2 * n + f).astype(f32).astype(bf16)
        width_rows[f] = jnp.dot(meta, pick, preferred_element_type=f32)

    def residual_step(c, window):
        @pl.when(c != me)
        def _():
            x_copy(c, me).wait_recv()
            halo_copy(c, me).wait_recv()

        first = pl.multiple_of(c * td, td)
        halo = jnp.dot(halo_all[c], spread[...], preferred_element_type=f32)
        keep = [keep_rows[rt, pl.ds(first, td), :] for rt in range(2)]
        scale = [scale_rows[rt, pl.ds(first, td), :] for rt in range(2)]
        window = list(window)
        pending = None
        for j in range(td):
            pixels = jnp.concatenate(
                [x_all[c, j].astype(f32), halo[:, j * LANES : (j + 1) * LANES]], axis=1
            )
            old = masked[first + j]
            values, residuals = [], []
            for rt in range(2):
                part = slice(rt * TILE_R, (rt + 1) * TILE_R)
                value = pixels[part] * keep[rt][j : j + 1]
                residuals.append(value - window[rt] * scale[rt][j : j + 1])
                window[rt] = window[rt] + (value - old[part])
                values.append(value)
            masked[first + j + HISTORY_FRAMES] = jnp.concatenate(values, axis=0)
            resid[c, j * rows : (j + 1) * rows, :] = jnp.concatenate(residuals, axis=0).astype(bf16)
            edge = jnp.where(core == 0, residuals[1], residuals[0])
            if j % 2 == 0:
                pending = edge
            else:
                at = (j // 2) * 2 * HALO_ROWS
                resid_out[c, at : at + 2 * HALO_ROWS, :] = jnp.concatenate(
                    [pending, edge], axis=0
                ).astype(bf16)
        row_copy(c).start()
        return tuple(window)

    blank = jnp.zeros((TILE_R, 2 * LANES), f32)
    lax.fori_loop(0, n, residual_step, (blank, blank))

    def filter_step(c, totals):
        row_copy(c).wait_recv()
        first = pl.multiple_of(c * td, td)
        excess, peak = list(totals[:2]), list(totals[2:])
        width = [width_rows[f, pl.ds(first, td), :] for f in range(2)]
        for j in range(td):
            for f in range(2):
                at = (2 * j + f) * rows
                chosen = jnp.broadcast_to(width[f][j : j + 1], (rows, 2 * LANES))
                row_w[at : at + rows, :] = pick_width(
                    chosen, [row_tab[s, j] for s in range(WIDTHS)]
                ).astype(bf16)
        row_result = jnp.dot(
            row_w[:, : td * (rows + HALO_ROWS)], resid[c], preferred_element_type=f32
        ).astype(bf16)
        trial = jnp.dot(row_result, col_tab[...], preferred_element_type=f32)
        for j in range(td):
            for f in range(2):
                at = (2 * j + f) * rows
                chosen = jnp.broadcast_to(width[f][j : j + 1, :LANES], (rows, LANES))
                filtered = pick_width(
                    chosen,
                    [
                        trial[at : at + rows, s * LANES : (s + 1) * LANES]
                        for s in range(WIDTHS)
                    ],
                )
                excess[f] = excess[f] + jnp.maximum(filtered - threshold, 0.0)
                peak[f] = jnp.maximum(peak[f], filtered)
        return tuple(excess) + tuple(peak)

    zero = jnp.zeros((rows, LANES), f32)
    low = jnp.full((rows, LANES), -1e30, f32)
    results = lax.fori_loop(0, n, filter_step, (zero, zero, low, low))
    for f in range(2):
        peak_out[f] = results[2 + f].astype(bf16)

    def send_peak(step, carry):
        peak_copy(me, peer(step)).start()
        return carry

    lax.fori_loop(1, n, send_peak, 0)
    peak_all[me] = peak_out[...]
    for f in range(2):
        exc_ref[f] = results[f] * (1.0 / total)

    def finish_sends(step, carry):
        target = peer(step)
        x_copy(me, target).wait_send()
        meta_copy(me, target).wait_send()
        halo_copy(me, target).wait_send()
        return carry

    lax.fori_loop(1, n, finish_sends, 0)

    def finish_rows(c, carry):
        row_copy(c).wait_send()
        return carry

    lax.fori_loop(0, n, finish_rows, 0)

    def finish_peaks(step, carry):
        source = peer(step)
        peak_copy(source, me).wait_recv()
        peak_copy(me, source).wait_send()
        return carry

    lax.fori_loop(1, n, finish_peaks, 0)
    for d in range(n):
        peak_ref[:, :, d * LANES : (d + 1) * LANES] = peak_all[d].astype(f32)


def fused_body(n, snapshots, tile_masks, widths):
    td, rows, cols = snapshots.shape
    total = n * td
    filters = widths.shape[1]
    flat = tile_masks.reshape(td, -1)
    meta = jnp.concatenate([flat, widths], axis=1).astype(jnp.float32)
    meta = jnp.pad(meta, ((0, 0), (0, LANES - meta.shape[1])))
    f32, bf16 = jnp.float32, jnp.bfloat16
    depth = td * (rows + HALO_ROWS)
    dma = pltpu.SemaphoreType.DMA((n,))
    return pl.pallas_call(
        functools.partial(search_kernel, n),
        out_shape=(
            jax.ShapeDtypeStruct((filters, rows, LANES), f32),
            jax.ShapeDtypeStruct((filters, rows, cols), f32),
        ),
        in_specs=[pl.BlockSpec(memory_space=pltpu.VMEM)] * 2,
        out_specs=(pl.BlockSpec(memory_space=pltpu.VMEM),) * 2,
        scratch_shapes=[
            pltpu.VMEM((n, td, rows, LANES), bf16),
            pltpu.VMEM((n, rows, LANES), bf16),
            pltpu.VMEM((n, rows, LANES), bf16),
            pltpu.VMEM((n, td, LANES), f32),
            pltpu.VMEM((2, total, 2 * LANES), f32),
            pltpu.VMEM((2, total, 2 * LANES), f32),
            pltpu.VMEM((filters, total, 2 * LANES), f32),
            pltpu.VMEM((total + HISTORY_FRAMES, rows, 2 * LANES), f32),
            pltpu.VMEM((n, depth, 2 * LANES), bf16),
            pltpu.VMEM((n, td * HALO_ROWS, 2 * LANES), bf16),
            pltpu.VMEM((td * filters * rows, 2 * LANES), bf16),
            pltpu.VMEM((WIDTHS, td, rows, 2 * LANES), f32),
            pltpu.VMEM((2 * LANES, WIDTHS * LANES), bf16),
            pltpu.VMEM((LANES, td * LANES), bf16),
            pltpu.VMEM((filters, rows, LANES), bf16),
            pltpu.VMEM((n, filters, rows, LANES), bf16),
        ]
        + [dma] * 10,
        compiler_params=pltpu.CompilerParams(
            collective_id=0, has_side_effects=True, vmem_limit_bytes=40 * 2**20
        ),
    )(snapshots, meta)


def solution(mesh):
    count = mesh.shape["tm"]

    def per_device(snapshots, tile_masks, widths):
        td, rows, cols = snapshots.shape
        fits = (
            mesh.shape["rows"] == 2
            and (td, rows, widths.shape[1]) == (8, 2 * TILE_R, 2)
            and cols == count * LANES
            and 2 * count + 2 <= LANES
        )
        if fits:
            return fused_body(count, snapshots, tile_masks, widths)
        return body(snapshots, tile_masks, widths)

    return jax.shard_map(
        per_device,
        mesh=mesh,
        in_specs=(P("tm", "rows", None), P("tm", "rows", None), P("tm", None)),
        out_specs=(P(None, "rows", "tm"), P(None, "rows", None)),
        check_vma=False,
    )
```

```python
import functools
import math

import jax
import jax.numpy as jnp
from jax import lax
from jax.experimental import pallas as pl
from jax.experimental.pallas import tpu as pltpu
from jax.sharding import PartitionSpec as P

HISTORY_FRAMES = 64
RADIUS = 8
TILE_R = 8
TILE_C = 128


threshold = 0.5


def padded(value, sides, width):
    for axis, dim in sides:
        count, length = (lax.axis_size(axis), value.shape[dim])
        up = [(i, (i + 1) % count) for i in range(count - 1)]
        down = [(j, i) for i, j in up]
        last = lax.slice_in_dim(value, length - width, length, axis=dim)
        first = lax.slice_in_dim(value, 0, width, axis=dim)
        before = lax.ppermute(last, axis, up)
        after = lax.ppermute(first, axis, down)
        value = jnp.concatenate([before, value, after], axis=dim)
    return value


def filter_taps(widths):
    sigma_val = widths.astype(jnp.float32)[..., None]
    offsets = jnp.arange(-RADIUS, RADIUS + 1).astype(jnp.float32)
    weights = jnp.exp(-(offsets * offsets) / (2.0 * sigma_val * sigma_val))
    return (weights / jnp.sqrt(jnp.sum(weights * weights, axis=-1, keepdims=True))).astype(
        jnp.bfloat16
    )


def history_band(local_times, back_step):
    target = jnp.arange(local_times)[:, None]
    source = jnp.arange(local_times)[None, :]
    distance = back_step * local_times + target - source
    return ((distance >= 1) & (distance <= HISTORY_FRAMES)).astype(jnp.bfloat16)


def tap_onehot(target_count):
    taps_count = 2 * RADIUS + 1
    source = jnp.arange(target_count + 2 * RADIUS)[:, None, None]
    target = jnp.arange(target_count)[None, :, None]
    return (source - target == jnp.arange(taps_count)[None, None, :]).astype(jnp.float32)


def column_residual(snapshots, tile_masks, widths):
    moved = lax.all_to_all(snapshots, "tm", split_axis=2, concat_axis=0, tiled=True)
    all_masks, all_widths = (
        lax.all_gather(tile_masks, "tm", axis=0, tiled=True),
        lax.all_gather(widths, "tm", axis=0, tiled=True),
    )
    total_times, local_rows, own_cols = moved.shape
    patch_rows = all_masks.shape[1]
    first_col = lax.axis_index("tm") * own_cols
    tile_of = (first_col + jnp.arange(own_cols)) // TILE_C
    pick = (jnp.arange(all_masks.shape[2])[:, None] == tile_of[None, :]).astype(jnp.float32)
    keep_tiles = jnp.einsum("trk,kc->trc", all_masks.astype(jnp.float32), pick)
    keep_pixels = jnp.broadcast_to(
        keep_tiles[:, :, None, :], (total_times, patch_rows, TILE_R, own_cols)
    ).reshape(total_times, local_rows, own_cols)
    pixels = local_rows * own_cols
    keep_flat = keep_pixels.astype(jnp.bfloat16).reshape(total_times, pixels)
    masked = moved.reshape(total_times, pixels) * keep_flat
    block_count = total_times // HISTORY_FRAMES
    own_band = history_band(HISTORY_FRAMES, 0)
    back_band = history_band(HISTORY_FRAMES, 1)
    empty_block = jnp.zeros((1, HISTORY_FRAMES, pixels), jnp.bfloat16)
    value_blocks = masked.reshape(block_count, HISTORY_FRAMES, pixels)
    keep_blocks = keep_flat.reshape(block_count, HISTORY_FRAMES, pixels)
    value_prior = jnp.concatenate([empty_block, value_blocks[:-1]], axis=0)
    keep_prior = jnp.concatenate([empty_block, keep_blocks[:-1]], axis=0)
    window = jnp.einsum("js,bsp->bjp", own_band, value_blocks, preferred_element_type=jnp.float32)
    window = window + jnp.einsum(
        "js,bsp->bjp", back_band, value_prior, preferred_element_type=jnp.float32
    )
    counts = jnp.einsum("js,bsp->bjp", own_band, keep_blocks, preferred_element_type=jnp.float32)
    counts = counts + jnp.einsum(
        "js,bsp->bjp", back_band, keep_prior, preferred_element_type=jnp.float32
    )
    mean_img = (window / jnp.maximum(counts, 1.0)).reshape(total_times, local_rows, own_cols)
    residual = (keep_pixels * (moved.astype(jnp.float32) - mean_img)).astype(jnp.bfloat16)
    return (residual, filter_taps(all_widths).astype(jnp.float32))


def body(snapshots, tile_masks, widths):
    residual, kernel = column_residual(snapshots, tile_masks, widths)
    local_times, local_rows, column_count = residual.shape
    padded_rows = padded(residual, (("rows", 1),), RADIUS)
    row_onehot = tap_onehot(local_rows)
    row_results = []
    for filter_index in range(widths.shape[1]):
        row_weights = jnp.einsum(
            "jik,tk->tij", row_onehot, kernel[:, filter_index], precision=lax.Precision.HIGHEST
        ).astype(jnp.bfloat16)
        row_results.append(
            jnp.einsum(
                "tij,tjc->tic", row_weights, padded_rows, preferred_element_type=jnp.float32
            ).astype(jnp.bfloat16)
        )
    stacked_rows = jnp.stack(row_results)
    padded_cols = padded(stacked_rows, (("tm", 3),), RADIUS)
    column_onehot = tap_onehot(column_count)
    excess_terms = []
    peak_terms = []
    for filter_index in range(widths.shape[1]):
        column_weights = jnp.einsum(
            "jck,tk->tjc", column_onehot, kernel[:, filter_index], precision=lax.Precision.HIGHEST
        ).astype(jnp.bfloat16)
        filtered = jnp.einsum(
            "trj,tjc->trc",
            padded_cols[filter_index],
            column_weights,
            preferred_element_type=jnp.float32,
        )
        excess_terms.append(jnp.sum(jnp.maximum(filtered - threshold, 0.0), axis=0))
        peak_terms.append(jnp.max(filtered, axis=0))
    excess_map = jnp.stack(excess_terms) / local_times
    peak_map = lax.all_gather(jnp.stack(peak_terms), "tm", axis=2, tiled=True)
    return (excess_map, peak_map)


MESH = pl.DeviceIdType.MESH
WIDTHS = 4
LANES = 128
HALO_ROWS = 8


def tap_values(offset, width):
    norm = math.sqrt(sum(math.exp(-(k * k) / (width * width)) for k in range(-RADIUS, RADIUS + 1)))
    value = jnp.exp(offset * offset * (-1.0 / (2.0 * width * width))) / norm
    return jnp.where(jnp.abs(offset) <= RADIUS, value, 0.0)


def pick_width(width, options):
    first, second, third, fourth = options
    return jnp.where(
        width == 1.0,
        first,
        jnp.where(width == 2.0, second, jnp.where(width == 3.0, third, fourth)),
    )


def search_kernel(
    n,
    x_hbm,
    flags_ref,
    widths_ref,
    exc_ref,
    peak_ref,
    x_ref,
    meta_ref,
    x_all,
    halo_out,
    halo_all,
    meta_all,
    keep_rows,
    scale_rows,
    width_rows,
    masked,
    resid,
    resid_out,
    row_w,
    row_tab,
    col_tab,
    spread,
    peak_out,
    peak_all,
    x_send,
    x_recv,
    meta_send,
    meta_recv,
    halo_send,
    halo_recv,
    row_send,
    row_recv,
    peak_send,
    peak_recv,
    load_sem,
):
    me, core = lax.axis_index("tm"), lax.axis_index("rows")
    td = x_ref.shape[0]
    rows = x_ref.shape[1]
    total = n * td
    f32, bf16 = jnp.float32, jnp.bfloat16

    def peer(step):
        return lax.rem(me + n - step, n)

    def lanes_of(band):
        return pl.ds(pl.multiple_of(band * LANES, LANES), LANES)

    def x_copy(source, target):
        return pltpu.make_async_remote_copy(
            src_ref=x_ref.at[:, :, lanes_of(target)],
            dst_ref=x_all.at[source],
            send_sem=x_send.at[target],
            recv_sem=x_recv.at[source],
            device_id={"tm": target},
            device_id_type=MESH,
        )

    def meta_copy(source, target):
        return pltpu.make_async_remote_copy(
            src_ref=meta_ref,
            dst_ref=meta_all.at[source],
            send_sem=meta_send.at[target],
            recv_sem=meta_recv.at[source],
            device_id={"tm": target},
            device_id_type=MESH,
        )

    def halo_copy(source, target):
        return pltpu.make_async_remote_copy(
            src_ref=halo_out.at[target],
            dst_ref=halo_all.at[source],
            send_sem=halo_send.at[target],
            recv_sem=halo_recv.at[source],
            device_id={"tm": target},
            device_id_type=MESH,
        )

    def row_copy(chunk):
        return pltpu.make_async_remote_copy(
            src_ref=resid_out.at[chunk],
            dst_ref=resid.at[chunk, pl.ds(td * rows, td * HALO_ROWS)],
            send_sem=row_send.at[chunk],
            recv_sem=row_recv.at[chunk],
            device_id={"rows": 1 - core},
            device_id_type=MESH,
        )

    def peak_copy(source, target):
        return pltpu.make_async_remote_copy(
            src_ref=peak_out,
            dst_ref=peak_all.at[source],
            send_sem=peak_send.at[target],
            recv_sem=peak_recv.at[source],
            device_id={"tm": target},
            device_id_type=MESH,
        )

    load = pltpu.make_async_copy(x_hbm, x_ref, load_sem)
    load.start()
    barrier = pltpu.get_barrier_semaphore()

    def greet(step, carry):
        pl.semaphore_signal(barrier, inc=1, device_id={"tm": peer(step)}, device_id_type=MESH)
        return carry

    lax.fori_loop(1, n, greet, 0)
    pl.semaphore_signal(barrier, inc=1, device_id={"rows": 1 - core}, device_id_type=MESH)
    meta_ref[...] = jnp.zeros_like(meta_ref)
    for j in range(td):
        for rt in range(2):
            meta_ref[j : j + 1, rt * n : (rt + 1) * n] = flags_ref[j, rt : rt + 1, :].astype(f32)
    meta_ref[:, 2 * n : 2 * n + 2] = widths_ref[...].astype(f32)
    load.wait()
    pl.semaphore_wait(barrier, n)

    def send_first(step, carry):
        meta_copy(me, peer(step)).start()
        x_copy(me, peer(step)).start()
        return carry

    lax.fori_loop(1, n, send_first, 0)

    side = 2 * RADIUS
    lane_in = lax.broadcasted_iota(jnp.int32, (LANES, 2 * LANES), 0)
    lane_out = lax.broadcasted_iota(jnp.int32, (LANES, 2 * LANES), 1)
    packed = jnp.zeros((n * rows, 2 * LANES), f32)
    for j in range(td):
        tiles = jnp.concatenate(
            [x_ref[j, :, d * LANES : (d + 1) * LANES] for d in range(n)], axis=0
        )
        to_right = (lane_in >= LANES - RADIUS) & (
            lane_out == lane_in - (LANES - RADIUS) + side * j
        )
        to_left = (lane_in < RADIUS) & (lane_out == LANES + lane_in + RADIUS + side * j)
        packed = packed + jnp.dot(
            tiles, (to_right | to_left).astype(f32).astype(bf16), preferred_element_type=f32
        )
    for d in range(n):
        tile = jnp.zeros((rows, LANES), f32)
        if d > 0:
            tile = tile + packed[(d - 1) * rows : d * rows, :LANES]
        if d < n - 1:
            tile = tile + packed[(d + 1) * rows : (d + 2) * rows, LANES:]
        halo_out[d] = tile.astype(bf16)

    def send_halo(step, carry):
        halo_copy(me, peer(step)).start()
        return carry

    lax.fori_loop(1, n, send_halo, 0)
    meta_all[me] = meta_ref[...]
    halo_all[me] = halo_out[me]
    x_all[me] = x_ref[:, :, lanes_of(me)]

    spread_in = lax.broadcasted_iota(jnp.int32, spread.shape, 0)
    spread_out = lax.broadcasted_iota(jnp.int32, spread.shape, 1)
    spread[...] = (
        (spread_out % LANES < side) & (spread_in == side * (spread_out // LANES) + spread_out % LANES)
    ).astype(f32).astype(bf16)
    lane = lax.broadcasted_iota(jnp.int32, (2 * LANES, LANES), 0)
    column = lax.broadcasted_iota(jnp.int32, (2 * LANES, LANES), 1)
    source_col = jnp.where(
        lane < LANES,
        lane,
        jnp.where(
            lane < LANES + RADIUS,
            lane - LANES - RADIUS,
            jnp.where(lane < LANES + side, lane - RADIUS, 4 * LANES),
        ),
    )
    column_offset = (source_col - column).astype(f32)
    for s in range(WIDTHS):
        col_tab[:, s * LANES : (s + 1) * LANES] = tap_values(column_offset, s + 1).astype(bf16)
    out_row = lax.broadcasted_iota(jnp.int32, (rows, 2 * LANES), 0)
    lane = lax.broadcasted_iota(jnp.int32, (rows, 2 * LANES), 1)
    own = lane < td * rows
    beside = lane - td * rows
    time_of = jnp.where(own, lane // rows, beside // HALO_ROWS)
    source_row = jnp.where(own, lane % rows, beside % HALO_ROWS + jnp.where(core == 0, rows, -HALO_ROWS))
    row_offset = (source_row - out_row).astype(f32)
    for s in range(WIDTHS):
        values = tap_values(row_offset, s + 1).astype(bf16).astype(f32)
        for j in range(td):
            row_tab[s, j] = jnp.where(time_of == j, values, 0.0)
    masked[0:HISTORY_FRAMES] = jnp.zeros((HISTORY_FRAMES,) + masked.shape[1:], f32)

    def wait_meta(step, carry):
        meta_copy(peer(step), me).wait_recv()
        return carry

    lax.fori_loop(1, n, wait_meta, 0)
    meta = meta_all[...].reshape(total, LANES).astype(bf16)
    entry = lax.broadcasted_iota(jnp.int32, (LANES, 2 * LANES), 0)
    lane = lax.broadcasted_iota(jnp.int32, (LANES, 2 * LANES), 1)
    tile_of = jnp.where(
        lane < LANES,
        me,
        jnp.where(lane < LANES + RADIUS, me - 1, jnp.where(lane < LANES + side, me + 1, -1)),
    )
    inside = (tile_of >= 0) & (tile_of < n)
    target = lax.broadcasted_iota(jnp.int32, (total, total), 0)
    source = lax.broadcasted_iota(jnp.int32, (total, total), 1)
    band = ((target - source >= 1) & (target - source <= HISTORY_FRAMES)).astype(f32).astype(bf16)
    for rt in range(2):
        pick = (inside & (entry == rt * n + tile_of)).astype(f32).astype(bf16)
        keep = jnp.dot(meta, pick, preferred_element_type=f32)
        counts = jnp.dot(band, keep.astype(bf16), preferred_element_type=f32)
        keep_rows[rt] = keep
        scale_rows[rt] = keep / jnp.maximum(counts, 1.0)
    for f in range(2):
        pick = (entry == 2 * n + f).astype(f32).astype(bf16)
        width_rows[f] = jnp.dot(meta, pick, preferred_element_type=f32)

    def weight_step(c, carry):
        first = pl.multiple_of(c * td, td)
        width = [width_rows[f, pl.ds(first, td), :] for f in range(2)]
        for j in range(td):
            for f in range(2):
                at = (2 * j + f) * rows
                chosen = jnp.broadcast_to(width[f][j : j + 1], (rows, 2 * LANES))
                row_w[c, at : at + rows, :] = pick_width(
                    chosen, [row_tab[s, j] for s in range(WIDTHS)]
                ).astype(bf16)
        return carry

    lax.fori_loop(0, n, weight_step, 0)

    def residual_step(c, window):
        @pl.when(c != me)
        def _():
            x_copy(c, me).wait_recv()
            halo_copy(c, me).wait_recv()

        first = pl.multiple_of(c * td, td)
        halo = jnp.dot(halo_all[c], spread[...], preferred_element_type=f32)
        keep = [keep_rows[rt, pl.ds(first, td), :] for rt in range(2)]
        scale = [scale_rows[rt, pl.ds(first, td), :] for rt in range(2)]
        window = list(window)
        pending = None
        for j in range(td):
            pixels = jnp.concatenate(
                [x_all[c, j].astype(f32), halo[:, j * LANES : (j + 1) * LANES]], axis=1
            )
            old = masked[first + j]
            values, residuals = [], []
            for rt in range(2):
                part = slice(rt * TILE_R, (rt + 1) * TILE_R)
                value = pixels[part] * keep[rt][j : j + 1]
                residuals.append(value - window[rt] * scale[rt][j : j + 1])
                window[rt] = window[rt] + (value - old[part])
                values.append(value)
            masked[first + j + HISTORY_FRAMES] = jnp.concatenate(values, axis=0)
            resid[c, j * rows : (j + 1) * rows, :] = jnp.concatenate(residuals, axis=0).astype(bf16)
            edge = jnp.where(core == 0, residuals[1], residuals[0])
            if j % 2 == 0:
                pending = edge
            else:
                at = (j // 2) * 2 * HALO_ROWS
                resid_out[c, at : at + 2 * HALO_ROWS, :] = jnp.concatenate(
                    [pending, edge], axis=0
                ).astype(bf16)
        row_copy(c).start()
        return tuple(window)

    blank = jnp.zeros((TILE_R, 2 * LANES), f32)
    window = residual_step(0, (blank, blank))

    def filter_step(c, totals):
        row_copy(c).wait_recv()
        first = pl.multiple_of(c * td, td)
        excess, peak = list(totals[:2]), list(totals[2:])
        width = [width_rows[f, pl.ds(first, td), :] for f in range(2)]
        row_result = jnp.dot(
            row_w[c, :, : td * (rows + HALO_ROWS)], resid[c], preferred_element_type=f32
        ).astype(bf16)
        trial = jnp.dot(row_result, col_tab[...], preferred_element_type=f32)
        for j in range(td):
            for f in range(2):
                at = (2 * j + f) * rows
                chosen = jnp.broadcast_to(width[f][j : j + 1, :LANES], (rows, LANES))
                filtered = pick_width(
                    chosen,
                    [
                        trial[at : at + rows, s * LANES : (s + 1) * LANES]
                        for s in range(WIDTHS)
                    ],
                )
                excess[f] = excess[f] + jnp.maximum(filtered - threshold, 0.0)
                peak[f] = jnp.maximum(peak[f], filtered)
        return tuple(excess) + tuple(peak)

    zero = jnp.zeros((rows, LANES), f32)
    low = jnp.full((rows, LANES), -1e30, f32)

    def both(c, carry):
        window = residual_step(c, carry[:2])
        return window + filter_step(c - 1, carry[2:])

    carry = lax.fori_loop(1, n, both, window + (zero, zero, low, low))
    results = filter_step(n - 1, carry[2:])
    for f in range(2):
        peak_out[f] = results[2 + f].astype(bf16)

    def send_peak(step, carry):
        peak_copy(me, peer(step)).start()
        return carry

    lax.fori_loop(1, n, send_peak, 0)
    peak_all[me] = peak_out[...]
    for f in range(2):
        exc_ref[f] = results[f] * (1.0 / total)

    def finish_sends(step, carry):
        target = peer(step)
        x_copy(me, target).wait_send()
        meta_copy(me, target).wait_send()
        halo_copy(me, target).wait_send()
        return carry

    lax.fori_loop(1, n, finish_sends, 0)

    def finish_rows(c, carry):
        row_copy(c).wait_send()
        return carry

    lax.fori_loop(0, n, finish_rows, 0)

    def finish_peaks(step, carry):
        source = peer(step)
        peak_copy(source, me).wait_recv()
        peak_copy(me, source).wait_send()
        return carry

    lax.fori_loop(1, n, finish_peaks, 0)
    for d in range(n):
        peak_ref[:, :, d * LANES : (d + 1) * LANES] = peak_all[d].astype(f32)


def fused_body(n, snapshots, tile_masks, widths):
    td, rows, cols = snapshots.shape
    total = n * td
    filters = widths.shape[1]
    f32, bf16 = jnp.float32, jnp.bfloat16
    depth = td * (rows + HALO_ROWS)
    dma = pltpu.SemaphoreType.DMA((n,))
    return pl.pallas_call(
        functools.partial(search_kernel, n),
        out_shape=(
            jax.ShapeDtypeStruct((filters, rows, LANES), f32),
            jax.ShapeDtypeStruct((filters, rows, cols), f32),
        ),
        in_specs=[
            pl.BlockSpec(memory_space=pl.ANY),
            pl.BlockSpec(memory_space=pltpu.VMEM),
            pl.BlockSpec(memory_space=pltpu.VMEM),
        ],
        out_specs=(pl.BlockSpec(memory_space=pltpu.VMEM),) * 2,
        scratch_shapes=[
            pltpu.VMEM((td, rows, cols), bf16),
            pltpu.VMEM((td, LANES), f32),
            pltpu.VMEM((n, td, rows, LANES), bf16),
            pltpu.VMEM((n, rows, LANES), bf16),
            pltpu.VMEM((n, rows, LANES), bf16),
            pltpu.VMEM((n, td, LANES), f32),
            pltpu.VMEM((2, total, 2 * LANES), f32),
            pltpu.VMEM((2, total, 2 * LANES), f32),
            pltpu.VMEM((filters, total, 2 * LANES), f32),
            pltpu.VMEM((total + HISTORY_FRAMES, rows, 2 * LANES), f32),
            pltpu.VMEM((n, depth, 2 * LANES), bf16),
            pltpu.VMEM((n, td * HALO_ROWS, 2 * LANES), bf16),
            pltpu.VMEM((n, td * filters * rows, 2 * LANES), bf16),
            pltpu.VMEM((WIDTHS, td, rows, 2 * LANES), f32),
            pltpu.VMEM((2 * LANES, WIDTHS * LANES), bf16),
            pltpu.VMEM((LANES, td * LANES), bf16),
            pltpu.VMEM((filters, rows, LANES), bf16),
            pltpu.VMEM((n, filters, rows, LANES), bf16),
        ]
        + [dma] * 10
        + [pltpu.SemaphoreType.DMA],
        compiler_params=pltpu.CompilerParams(
            collective_id=0, has_side_effects=True, vmem_limit_bytes=40 * 2**20
        ),
    )(snapshots, tile_masks, widths)


def solution(mesh):
    count = mesh.shape["tm"]

    def per_device(snapshots, tile_masks, widths):
        td, rows, cols = snapshots.shape
        fits = (
            mesh.shape["rows"] == 2
            and (td, rows, widths.shape[1]) == (8, 2 * TILE_R, 2)
            and cols == count * LANES
            and 2 * count + 2 <= LANES
        )
        if fits:
            return fused_body(count, snapshots, tile_masks, widths)
        return body(snapshots, tile_masks, widths)

    return jax.shard_map(
        per_device,
        mesh=mesh,
        in_specs=(P("tm", "rows", None), P("tm", "rows", None), P("tm", None)),
        out_specs=(P(None, "rows", "tm"), P(None, "rows", None)),
        check_vma=False,
    )
```

```python
import functools
import math

import jax
import jax.numpy as jnp
from jax import lax
from jax.experimental import pallas as pl
from jax.experimental.pallas import tpu as pltpu
from jax.sharding import PartitionSpec as P

HISTORY_FRAMES = 64
RADIUS = 8
TILE_R = 8
TILE_C = 128


threshold = 0.5


def padded(value, sides, width):
    for axis, dim in sides:
        count, length = (lax.axis_size(axis), value.shape[dim])
        up = [(i, (i + 1) % count) for i in range(count - 1)]
        down = [(j, i) for i, j in up]
        last = lax.slice_in_dim(value, length - width, length, axis=dim)
        first = lax.slice_in_dim(value, 0, width, axis=dim)
        before = lax.ppermute(last, axis, up)
        after = lax.ppermute(first, axis, down)
        value = jnp.concatenate([before, value, after], axis=dim)
    return value


def filter_taps(widths):
    sigma_val = widths.astype(jnp.float32)[..., None]
    offsets = jnp.arange(-RADIUS, RADIUS + 1).astype(jnp.float32)
    weights = jnp.exp(-(offsets * offsets) / (2.0 * sigma_val * sigma_val))
    return (weights / jnp.sqrt(jnp.sum(weights * weights, axis=-1, keepdims=True))).astype(
        jnp.bfloat16
    )


def history_band(local_times, back_step):
    target = jnp.arange(local_times)[:, None]
    source = jnp.arange(local_times)[None, :]
    distance = back_step * local_times + target - source
    return ((distance >= 1) & (distance <= HISTORY_FRAMES)).astype(jnp.bfloat16)


def tap_onehot(target_count):
    taps_count = 2 * RADIUS + 1
    source = jnp.arange(target_count + 2 * RADIUS)[:, None, None]
    target = jnp.arange(target_count)[None, :, None]
    return (source - target == jnp.arange(taps_count)[None, None, :]).astype(jnp.float32)


def column_residual(snapshots, tile_masks, widths):
    moved = lax.all_to_all(snapshots, "tm", split_axis=2, concat_axis=0, tiled=True)
    all_masks, all_widths = (
        lax.all_gather(tile_masks, "tm", axis=0, tiled=True),
        lax.all_gather(widths, "tm", axis=0, tiled=True),
    )
    total_times, local_rows, own_cols = moved.shape
    patch_rows = all_masks.shape[1]
    first_col = lax.axis_index("tm") * own_cols
    tile_of = (first_col + jnp.arange(own_cols)) // TILE_C
    pick = (jnp.arange(all_masks.shape[2])[:, None] == tile_of[None, :]).astype(jnp.float32)
    keep_tiles = jnp.einsum("trk,kc->trc", all_masks.astype(jnp.float32), pick)
    keep_pixels = jnp.broadcast_to(
        keep_tiles[:, :, None, :], (total_times, patch_rows, TILE_R, own_cols)
    ).reshape(total_times, local_rows, own_cols)
    pixels = local_rows * own_cols
    keep_flat = keep_pixels.astype(jnp.bfloat16).reshape(total_times, pixels)
    masked = moved.reshape(total_times, pixels) * keep_flat
    block_count = total_times // HISTORY_FRAMES
    own_band = history_band(HISTORY_FRAMES, 0)
    back_band = history_band(HISTORY_FRAMES, 1)
    empty_block = jnp.zeros((1, HISTORY_FRAMES, pixels), jnp.bfloat16)
    value_blocks = masked.reshape(block_count, HISTORY_FRAMES, pixels)
    keep_blocks = keep_flat.reshape(block_count, HISTORY_FRAMES, pixels)
    value_prior = jnp.concatenate([empty_block, value_blocks[:-1]], axis=0)
    keep_prior = jnp.concatenate([empty_block, keep_blocks[:-1]], axis=0)
    window = jnp.einsum("js,bsp->bjp", own_band, value_blocks, preferred_element_type=jnp.float32)
    window = window + jnp.einsum(
        "js,bsp->bjp", back_band, value_prior, preferred_element_type=jnp.float32
    )
    counts = jnp.einsum("js,bsp->bjp", own_band, keep_blocks, preferred_element_type=jnp.float32)
    counts = counts + jnp.einsum(
        "js,bsp->bjp", back_band, keep_prior, preferred_element_type=jnp.float32
    )
    mean_img = (window / jnp.maximum(counts, 1.0)).reshape(total_times, local_rows, own_cols)
    residual = (keep_pixels * (moved.astype(jnp.float32) - mean_img)).astype(jnp.bfloat16)
    return (residual, filter_taps(all_widths).astype(jnp.float32))


def body(snapshots, tile_masks, widths):
    residual, kernel = column_residual(snapshots, tile_masks, widths)
    local_times, local_rows, column_count = residual.shape
    padded_rows = padded(residual, (("rows", 1),), RADIUS)
    row_onehot = tap_onehot(local_rows)
    row_results = []
    for filter_index in range(widths.shape[1]):
        row_weights = jnp.einsum(
            "jik,tk->tij", row_onehot, kernel[:, filter_index], precision=lax.Precision.HIGHEST
        ).astype(jnp.bfloat16)
        row_results.append(
            jnp.einsum(
                "tij,tjc->tic", row_weights, padded_rows, preferred_element_type=jnp.float32
            ).astype(jnp.bfloat16)
        )
    stacked_rows = jnp.stack(row_results)
    padded_cols = padded(stacked_rows, (("tm", 3),), RADIUS)
    column_onehot = tap_onehot(column_count)
    excess_terms = []
    peak_terms = []
    for filter_index in range(widths.shape[1]):
        column_weights = jnp.einsum(
            "jck,tk->tjc", column_onehot, kernel[:, filter_index], precision=lax.Precision.HIGHEST
        ).astype(jnp.bfloat16)
        filtered = jnp.einsum(
            "trj,tjc->trc",
            padded_cols[filter_index],
            column_weights,
            preferred_element_type=jnp.float32,
        )
        excess_terms.append(jnp.sum(jnp.maximum(filtered - threshold, 0.0), axis=0))
        peak_terms.append(jnp.max(filtered, axis=0))
    excess_map = jnp.stack(excess_terms) / local_times
    peak_map = lax.all_gather(jnp.stack(peak_terms), "tm", axis=2, tiled=True)
    return (excess_map, peak_map)


MESH = pl.DeviceIdType.MESH
WIDTHS = 4
LANES = 128
HALO_ROWS = 8


def tap_values(offset, width):
    norm = math.sqrt(sum(math.exp(-(k * k) / (width * width)) for k in range(-RADIUS, RADIUS + 1)))
    value = jnp.exp(offset * offset * (-1.0 / (2.0 * width * width))) / norm
    return jnp.where(jnp.abs(offset) <= RADIUS, value, 0.0)


def pick_width(width, options):
    first, second, third, fourth = options
    return jnp.where(
        width == 1.0,
        first,
        jnp.where(width == 2.0, second, jnp.where(width == 3.0, third, fourth)),
    )


def search_kernel(
    n,
    x_ref,
    meta_ref,
    exc_ref,
    peak_ref,
    x_all,
    halo_out,
    halo_all,
    meta_all,
    keep_rows,
    scale_rows,
    width_rows,
    masked,
    resid,
    resid_out,
    row_w,
    row_tab,
    col_tab,
    spread,
    peak_out,
    peak_all,
    x_send,
    x_recv,
    meta_send,
    meta_recv,
    halo_send,
    halo_recv,
    row_send,
    row_recv,
    peak_send,
    peak_recv,
):
    me, core = lax.axis_index("tm"), lax.axis_index("rows")
    td = x_ref.shape[0]
    rows = x_ref.shape[1]
    total = n * td
    f32, bf16 = jnp.float32, jnp.bfloat16

    def peer(step):
        return lax.rem(me + n - step, n)

    def lanes_of(band):
        return pl.ds(pl.multiple_of(band * LANES, LANES), LANES)

    def x_copy(source, target):
        return pltpu.make_async_remote_copy(
            src_ref=x_ref.at[:, :, lanes_of(target)],
            dst_ref=x_all.at[source],
            send_sem=x_send.at[target],
            recv_sem=x_recv.at[source],
            device_id={"tm": target},
            device_id_type=MESH,
        )

    def meta_copy(source, target):
        return pltpu.make_async_remote_copy(
            src_ref=meta_ref,
            dst_ref=meta_all.at[source],
            send_sem=meta_send.at[target],
            recv_sem=meta_recv.at[source],
            device_id={"tm": target},
            device_id_type=MESH,
        )

    def halo_copy(source, target):
        return pltpu.make_async_remote_copy(
            src_ref=halo_out.at[target],
            dst_ref=halo_all.at[source],
            send_sem=halo_send.at[target],
            recv_sem=halo_recv.at[source],
            device_id={"tm": target},
            device_id_type=MESH,
        )

    def row_copy(chunk):
        return pltpu.make_async_remote_copy(
            src_ref=resid_out.at[chunk],
            dst_ref=resid.at[chunk, pl.ds(td * rows, td * HALO_ROWS)],
            send_sem=row_send.at[chunk],
            recv_sem=row_recv.at[chunk],
            device_id={"rows": 1 - core},
            device_id_type=MESH,
        )

    def peak_copy(source, target):
        return pltpu.make_async_remote_copy(
            src_ref=peak_out,
            dst_ref=peak_all.at[source],
            send_sem=peak_send.at[target],
            recv_sem=peak_recv.at[source],
            device_id={"tm": target},
            device_id_type=MESH,
        )

    barrier = pltpu.get_barrier_semaphore()

    def greet(step, carry):
        pl.semaphore_signal(barrier, inc=1, device_id={"tm": peer(step)}, device_id_type=MESH)
        return carry

    lax.fori_loop(1, n, greet, 0)
    pl.semaphore_signal(barrier, inc=1, device_id={"rows": 1 - core}, device_id_type=MESH)
    pl.semaphore_wait(barrier, n)

    def send_first(step, carry):
        meta_copy(me, peer(step)).start()
        x_copy(me, peer(step)).start()
        return carry

    lax.fori_loop(1, n, send_first, 0)

    side = 2 * RADIUS
    lane_in = lax.broadcasted_iota(jnp.int32, (LANES, 2 * LANES), 0)
    lane_out = lax.broadcasted_iota(jnp.int32, (LANES, 2 * LANES), 1)
    packed = jnp.zeros((n * rows, 2 * LANES), f32)
    for j in range(td):
        tiles = jnp.concatenate(
            [x_ref[j, :, d * LANES : (d + 1) * LANES] for d in range(n)], axis=0
        )
        to_right = (lane_in >= LANES - RADIUS) & (
            lane_out == lane_in - (LANES - RADIUS) + side * j
        )
        to_left = (lane_in < RADIUS) & (lane_out == LANES + lane_in + RADIUS + side * j)
        packed = packed + jnp.dot(
            tiles, (to_right | to_left).astype(f32).astype(bf16), preferred_element_type=f32
        )
    for d in range(n):
        tile = jnp.zeros((rows, LANES), f32)
        if d > 0:
            tile = tile + packed[(d - 1) * rows : d * rows, :LANES]
        if d < n - 1:
            tile = tile + packed[(d + 1) * rows : (d + 2) * rows, LANES:]
        halo_out[d] = tile.astype(bf16)

    def send_halo(step, carry):
        halo_copy(me, peer(step)).start()
        return carry

    lax.fori_loop(1, n, send_halo, 0)
    meta_all[me] = meta_ref[...]
    halo_all[me] = halo_out[me]
    x_all[me] = x_ref[:, :, lanes_of(me)]

    spread_in = lax.broadcasted_iota(jnp.int32, spread.shape, 0)
    spread_out = lax.broadcasted_iota(jnp.int32, spread.shape, 1)
    spread[...] = (
        (spread_out % LANES < side) & (spread_in == side * (spread_out // LANES) + spread_out % LANES)
    ).astype(f32).astype(bf16)
    lane = lax.broadcasted_iota(jnp.int32, (2 * LANES, LANES), 0)
    column = lax.broadcasted_iota(jnp.int32, (2 * LANES, LANES), 1)
    source_col = jnp.where(
        lane < LANES,
        lane,
        jnp.where(
            lane < LANES + RADIUS,
            lane - LANES - RADIUS,
            jnp.where(lane < LANES + side, lane - RADIUS, 4 * LANES),
        ),
    )
    column_offset = (source_col - column).astype(f32)
    for s in range(WIDTHS):
        col_tab[:, s * LANES : (s + 1) * LANES] = tap_values(column_offset, s + 1).astype(bf16)
    out_row = lax.broadcasted_iota(jnp.int32, (rows, 2 * LANES), 0)
    lane = lax.broadcasted_iota(jnp.int32, (rows, 2 * LANES), 1)
    own = lane < td * rows
    beside = lane - td * rows
    time_of = jnp.where(own, lane // rows, beside // HALO_ROWS)
    source_row = jnp.where(own, lane % rows, beside % HALO_ROWS + jnp.where(core == 0, rows, -HALO_ROWS))
    row_offset = (source_row - out_row).astype(f32)
    for s in range(WIDTHS):
        values = tap_values(row_offset, s + 1).astype(bf16).astype(f32)
        for j in range(td):
            row_tab[s, j] = jnp.where(time_of == j, values, 0.0)
    masked[0:HISTORY_FRAMES] = jnp.zeros((HISTORY_FRAMES,) + masked.shape[1:], f32)

    def wait_meta(step, carry):
        meta_copy(peer(step), me).wait_recv()
        return carry

    lax.fori_loop(1, n, wait_meta, 0)
    meta = meta_all[...].reshape(total, LANES).astype(bf16)
    entry = lax.broadcasted_iota(jnp.int32, (LANES, 2 * LANES), 0)
    lane = lax.broadcasted_iota(jnp.int32, (LANES, 2 * LANES), 1)
    tile_of = jnp.where(
        lane < LANES,
        me,
        jnp.where(lane < LANES + RADIUS, me - 1, jnp.where(lane < LANES + side, me + 1, -1)),
    )
    inside = (tile_of >= 0) & (tile_of < n)
    target = lax.broadcasted_iota(jnp.int32, (total, total), 0)
    source = lax.broadcasted_iota(jnp.int32, (total, total), 1)
    band = ((target - source >= 1) & (target - source <= HISTORY_FRAMES)).astype(f32).astype(bf16)
    for rt in range(2):
        pick = (inside & (entry == rt * n + tile_of)).astype(f32).astype(bf16)
        keep = jnp.dot(meta, pick, preferred_element_type=f32)
        counts = jnp.dot(band, keep.astype(bf16), preferred_element_type=f32)
        keep_rows[rt] = keep
        scale_rows[rt] = keep / jnp.maximum(counts, 1.0)
    for f in range(2):
        pick = (entry == 2 * n + f).astype(f32).astype(bf16)
        width_rows[f] = jnp.dot(meta, pick, preferred_element_type=f32)

    def weight_step(c, carry):
        first = pl.multiple_of(c * td, td)
        width = [width_rows[f, pl.ds(first, td), :] for f in range(2)]
        for j in range(td):
            for f in range(2):
                at = (2 * j + f) * rows
                chosen = jnp.broadcast_to(width[f][j : j + 1], (rows, 2 * LANES))
                row_w[c, at : at + rows, :] = pick_width(
                    chosen, [row_tab[s, j] for s in range(WIDTHS)]
                ).astype(bf16)
        return carry

    lax.fori_loop(0, n, weight_step, 0)

    def residual_step(c, window):
        @pl.when(c != me)
        def _():
            x_copy(c, me).wait_recv()
            halo_copy(c, me).wait_recv()

        first = pl.multiple_of(c * td, td)
        halo = jnp.dot(halo_all[c], spread[...], preferred_element_type=f32)
        keep = [keep_rows[rt, pl.ds(first, td), :] for rt in range(2)]
        scale = [scale_rows[rt, pl.ds(first, td), :] for rt in range(2)]
        window = list(window)
        pending = None
        for j in range(td):
            pixels = jnp.concatenate(
                [x_all[c, j].astype(f32), halo[:, j * LANES : (j + 1) * LANES]], axis=1
            )
            old = masked[first + j]
            values, residuals = [], []
            for rt in range(2):
                part = slice(rt * TILE_R, (rt + 1) * TILE_R)
                value = pixels[part] * keep[rt][j : j + 1]
                residuals.append(value - window[rt] * scale[rt][j : j + 1])
                window[rt] = window[rt] + (value - old[part])
                values.append(value)
            masked[first + j + HISTORY_FRAMES] = jnp.concatenate(values, axis=0)
            resid[c, j * rows : (j + 1) * rows, :] = jnp.concatenate(residuals, axis=0).astype(bf16)
            edge = jnp.where(core == 0, residuals[1], residuals[0])
            if j % 2 == 0:
                pending = edge
            else:
                at = (j // 2) * 2 * HALO_ROWS
                resid_out[c, at : at + 2 * HALO_ROWS, :] = jnp.concatenate(
                    [pending, edge], axis=0
                ).astype(bf16)
        row_copy(c).start()
        return tuple(window)

    blank = jnp.zeros((TILE_R, 2 * LANES), f32)
    lax.fori_loop(0, n, residual_step, (blank, blank))

    def filter_step(g, totals):
        excess, peak = list(totals[:2]), list(totals[2:])
        row_results, width = [], []
        for part in range(group):
            c = g * group + part
            row_copy(c).wait_recv()
            first = pl.multiple_of(c * td, td)
            width.append([width_rows[f, pl.ds(first, td), :] for f in range(2)])
            row_results.append(
                jnp.dot(
                    row_w[c, :, : td * (rows + HALO_ROWS)], resid[c], preferred_element_type=f32
                ).astype(bf16)
            )
        trial = jnp.dot(
            jnp.concatenate(row_results, axis=0), col_tab[...], preferred_element_type=f32
        )
        for part in range(group):
            for j in range(td):
                for f in range(2):
                    at = ((part * td + j) * 2 + f) * rows
                    chosen = jnp.broadcast_to(width[part][f][j : j + 1, :LANES], (rows, LANES))
                    filtered = pick_width(
                        chosen,
                        [
                            trial[at : at + rows, s * LANES : (s + 1) * LANES]
                            for s in range(WIDTHS)
                        ],
                    )
                    excess[f] = excess[f] + jnp.maximum(filtered - threshold, 0.0)
                    peak[f] = jnp.maximum(peak[f], filtered)
        return tuple(excess) + tuple(peak)

    group = 4 if n % 4 == 0 else 1
    zero = jnp.zeros((rows, LANES), f32)
    low = jnp.full((rows, LANES), -1e30, f32)
    results = lax.fori_loop(0, n // group, filter_step, (zero, zero, low, low))
    for f in range(2):
        peak_out[f] = results[2 + f].astype(bf16)

    def send_peak(step, carry):
        peak_copy(me, peer(step)).start()
        return carry

    lax.fori_loop(1, n, send_peak, 0)
    peak_all[me] = peak_out[...]
    for f in range(2):
        exc_ref[f] = results[f] * (1.0 / total)

    def finish_sends(step, carry):
        target = peer(step)
        x_copy(me, target).wait_send()
        meta_copy(me, target).wait_send()
        halo_copy(me, target).wait_send()
        return carry

    lax.fori_loop(1, n, finish_sends, 0)

    def finish_rows(c, carry):
        row_copy(c).wait_send()
        return carry

    lax.fori_loop(0, n, finish_rows, 0)

    def finish_peaks(step, carry):
        source = peer(step)
        peak_copy(source, me).wait_recv()
        peak_copy(me, source).wait_send()
        return carry

    lax.fori_loop(1, n, finish_peaks, 0)
    for d in range(n):
        peak_ref[:, :, d * LANES : (d + 1) * LANES] = peak_all[d].astype(f32)


def fused_body(n, snapshots, tile_masks, widths):
    td, rows, cols = snapshots.shape
    total = n * td
    filters = widths.shape[1]
    flat = tile_masks.reshape(td, -1)
    meta = jnp.concatenate([flat, widths], axis=1).astype(jnp.float32)
    meta = jnp.pad(meta, ((0, 0), (0, LANES - meta.shape[1])))
    f32, bf16 = jnp.float32, jnp.bfloat16
    depth = td * (rows + HALO_ROWS)
    dma = pltpu.SemaphoreType.DMA((n,))
    return pl.pallas_call(
        functools.partial(search_kernel, n),
        out_shape=(
            jax.ShapeDtypeStruct((filters, rows, LANES), f32),
            jax.ShapeDtypeStruct((filters, rows, cols), f32),
        ),
        in_specs=[pl.BlockSpec(memory_space=pltpu.VMEM)] * 2,
        out_specs=(pl.BlockSpec(memory_space=pltpu.VMEM),) * 2,
        scratch_shapes=[
            pltpu.VMEM((n, td, rows, LANES), bf16),
            pltpu.VMEM((n, rows, LANES), bf16),
            pltpu.VMEM((n, rows, LANES), bf16),
            pltpu.VMEM((n, td, LANES), f32),
            pltpu.VMEM((2, total, 2 * LANES), f32),
            pltpu.VMEM((2, total, 2 * LANES), f32),
            pltpu.VMEM((filters, total, 2 * LANES), f32),
            pltpu.VMEM((total + HISTORY_FRAMES, rows, 2 * LANES), f32),
            pltpu.VMEM((n, depth, 2 * LANES), bf16),
            pltpu.VMEM((n, td * HALO_ROWS, 2 * LANES), bf16),
            pltpu.VMEM((n, td * filters * rows, 2 * LANES), bf16),
            pltpu.VMEM((WIDTHS, td, rows, 2 * LANES), f32),
            pltpu.VMEM((2 * LANES, WIDTHS * LANES), bf16),
            pltpu.VMEM((LANES, td * LANES), bf16),
            pltpu.VMEM((filters, rows, LANES), bf16),
            pltpu.VMEM((n, filters, rows, LANES), bf16),
        ]
        + [dma] * 10,
        compiler_params=pltpu.CompilerParams(
            collective_id=0, has_side_effects=True, vmem_limit_bytes=40 * 2**20
        ),
    )(snapshots, meta)


def solution(mesh):
    count = mesh.shape["tm"]

    def per_device(snapshots, tile_masks, widths):
        td, rows, cols = snapshots.shape
        fits = (
            mesh.shape["rows"] == 2
            and (td, rows, widths.shape[1]) == (8, 2 * TILE_R, 2)
            and cols == count * LANES
            and 2 * count + 2 <= LANES
        )
        if fits:
            return fused_body(count, snapshots, tile_masks, widths)
        return body(snapshots, tile_masks, widths)

    return jax.shard_map(
        per_device,
        mesh=mesh,
        in_specs=(P("tm", "rows", None), P("tm", "rows", None), P("tm", None)),
        out_specs=(P(None, "rows", "tm"), P(None, "rows", None)),
        check_vma=False,
    )
```

```python
import functools
import math

import jax
import jax.numpy as jnp
from jax import lax
from jax.experimental import pallas as pl
from jax.experimental.pallas import tpu as pltpu
from jax.sharding import PartitionSpec as P

HISTORY_FRAMES = 64
RADIUS = 8
TILE_R = 8
TILE_C = 128


threshold = 0.5


def padded(value, sides, width):
    for axis, dim in sides:
        count, length = (lax.axis_size(axis), value.shape[dim])
        up = [(i, (i + 1) % count) for i in range(count - 1)]
        down = [(j, i) for i, j in up]
        last = lax.slice_in_dim(value, length - width, length, axis=dim)
        first = lax.slice_in_dim(value, 0, width, axis=dim)
        before = lax.ppermute(last, axis, up)
        after = lax.ppermute(first, axis, down)
        value = jnp.concatenate([before, value, after], axis=dim)
    return value


def filter_taps(widths):
    sigma_val = widths.astype(jnp.float32)[..., None]
    offsets = jnp.arange(-RADIUS, RADIUS + 1).astype(jnp.float32)
    weights = jnp.exp(-(offsets * offsets) / (2.0 * sigma_val * sigma_val))
    return (weights / jnp.sqrt(jnp.sum(weights * weights, axis=-1, keepdims=True))).astype(
        jnp.bfloat16
    )


def history_band(local_times, back_step):
    target = jnp.arange(local_times)[:, None]
    source = jnp.arange(local_times)[None, :]
    distance = back_step * local_times + target - source
    return ((distance >= 1) & (distance <= HISTORY_FRAMES)).astype(jnp.bfloat16)


def tap_onehot(target_count):
    taps_count = 2 * RADIUS + 1
    source = jnp.arange(target_count + 2 * RADIUS)[:, None, None]
    target = jnp.arange(target_count)[None, :, None]
    return (source - target == jnp.arange(taps_count)[None, None, :]).astype(jnp.float32)


def column_residual(snapshots, tile_masks, widths):
    moved = lax.all_to_all(snapshots, "tm", split_axis=2, concat_axis=0, tiled=True)
    all_masks, all_widths = (
        lax.all_gather(tile_masks, "tm", axis=0, tiled=True),
        lax.all_gather(widths, "tm", axis=0, tiled=True),
    )
    total_times, local_rows, own_cols = moved.shape
    patch_rows = all_masks.shape[1]
    first_col = lax.axis_index("tm") * own_cols
    tile_of = (first_col + jnp.arange(own_cols)) // TILE_C
    pick = (jnp.arange(all_masks.shape[2])[:, None] == tile_of[None, :]).astype(jnp.float32)
    keep_tiles = jnp.einsum("trk,kc->trc", all_masks.astype(jnp.float32), pick)
    keep_pixels = jnp.broadcast_to(
        keep_tiles[:, :, None, :], (total_times, patch_rows, TILE_R, own_cols)
    ).reshape(total_times, local_rows, own_cols)
    pixels = local_rows * own_cols
    keep_flat = keep_pixels.astype(jnp.bfloat16).reshape(total_times, pixels)
    masked = moved.reshape(total_times, pixels) * keep_flat
    block_count = total_times // HISTORY_FRAMES
    own_band = history_band(HISTORY_FRAMES, 0)
    back_band = history_band(HISTORY_FRAMES, 1)
    empty_block = jnp.zeros((1, HISTORY_FRAMES, pixels), jnp.bfloat16)
    value_blocks = masked.reshape(block_count, HISTORY_FRAMES, pixels)
    keep_blocks = keep_flat.reshape(block_count, HISTORY_FRAMES, pixels)
    value_prior = jnp.concatenate([empty_block, value_blocks[:-1]], axis=0)
    keep_prior = jnp.concatenate([empty_block, keep_blocks[:-1]], axis=0)
    window = jnp.einsum("js,bsp->bjp", own_band, value_blocks, preferred_element_type=jnp.float32)
    window = window + jnp.einsum(
        "js,bsp->bjp", back_band, value_prior, preferred_element_type=jnp.float32
    )
    counts = jnp.einsum("js,bsp->bjp", own_band, keep_blocks, preferred_element_type=jnp.float32)
    counts = counts + jnp.einsum(
        "js,bsp->bjp", back_band, keep_prior, preferred_element_type=jnp.float32
    )
    mean_img = (window / jnp.maximum(counts, 1.0)).reshape(total_times, local_rows, own_cols)
    residual = (keep_pixels * (moved.astype(jnp.float32) - mean_img)).astype(jnp.bfloat16)
    return (residual, filter_taps(all_widths).astype(jnp.float32))


def body(snapshots, tile_masks, widths):
    residual, kernel = column_residual(snapshots, tile_masks, widths)
    local_times, local_rows, column_count = residual.shape
    padded_rows = padded(residual, (("rows", 1),), RADIUS)
    row_onehot = tap_onehot(local_rows)
    row_results = []
    for filter_index in range(widths.shape[1]):
        row_weights = jnp.einsum(
            "jik,tk->tij", row_onehot, kernel[:, filter_index], precision=lax.Precision.HIGHEST
        ).astype(jnp.bfloat16)
        row_results.append(
            jnp.einsum(
                "tij,tjc->tic", row_weights, padded_rows, preferred_element_type=jnp.float32
            ).astype(jnp.bfloat16)
        )
    stacked_rows = jnp.stack(row_results)
    padded_cols = padded(stacked_rows, (("tm", 3),), RADIUS)
    column_onehot = tap_onehot(column_count)
    excess_terms = []
    peak_terms = []
    for filter_index in range(widths.shape[1]):
        column_weights = jnp.einsum(
            "jck,tk->tjc", column_onehot, kernel[:, filter_index], precision=lax.Precision.HIGHEST
        ).astype(jnp.bfloat16)
        filtered = jnp.einsum(
            "trj,tjc->trc",
            padded_cols[filter_index],
            column_weights,
            preferred_element_type=jnp.float32,
        )
        excess_terms.append(jnp.sum(jnp.maximum(filtered - threshold, 0.0), axis=0))
        peak_terms.append(jnp.max(filtered, axis=0))
    excess_map = jnp.stack(excess_terms) / local_times
    peak_map = lax.all_gather(jnp.stack(peak_terms), "tm", axis=2, tiled=True)
    return (excess_map, peak_map)


MESH = pl.DeviceIdType.MESH
WIDTHS = 4
LANES = 128
HALO_ROWS = 8


def tap_values(offset, width):
    norm = math.sqrt(sum(math.exp(-(k * k) / (width * width)) for k in range(-RADIUS, RADIUS + 1)))
    value = jnp.exp(offset * offset * (-1.0 / (2.0 * width * width))) / norm
    return jnp.where(jnp.abs(offset) <= RADIUS, value, 0.0)


def pick_width(width, options):
    first, second, third, fourth = options
    return jnp.where(
        width == 1.0,
        first,
        jnp.where(width == 2.0, second, jnp.where(width == 3.0, third, fourth)),
    )


def search_kernel(
    n,
    x_ref,
    meta_ref,
    exc_ref,
    peak_ref,
    x_all,
    halo_out,
    halo_all,
    meta_all,
    keep_rows,
    scale_rows,
    width_rows,
    masked,
    resid,
    resid_out,
    row_w,
    row_tab,
    col_tab,
    spread,
    peak_out,
    peak_all,
    x_send,
    x_recv,
    meta_send,
    meta_recv,
    halo_send,
    halo_recv,
    row_send,
    row_recv,
    peak_send,
    peak_recv,
):
    me, core = lax.axis_index("tm"), lax.axis_index("rows")
    td = x_ref.shape[0]
    rows = x_ref.shape[1]
    total = n * td
    f32, bf16 = jnp.float32, jnp.bfloat16

    def peer(step):
        return lax.rem(me + n - step, n)

    def lanes_of(band):
        return pl.ds(pl.multiple_of(band * LANES, LANES), LANES)

    def x_copy(source, target):
        return pltpu.make_async_remote_copy(
            src_ref=x_ref.at[:, :, lanes_of(target)],
            dst_ref=x_all.at[source],
            send_sem=x_send.at[target],
            recv_sem=x_recv.at[source],
            device_id={"tm": target},
            device_id_type=MESH,
        )

    def meta_copy(source, target):
        return pltpu.make_async_remote_copy(
            src_ref=meta_ref,
            dst_ref=meta_all.at[source],
            send_sem=meta_send.at[target],
            recv_sem=meta_recv.at[source],
            device_id={"tm": target},
            device_id_type=MESH,
        )

    def halo_copy(source, target):
        return pltpu.make_async_remote_copy(
            src_ref=halo_out.at[target],
            dst_ref=halo_all.at[source],
            send_sem=halo_send.at[target],
            recv_sem=halo_recv.at[source],
            device_id={"tm": target},
            device_id_type=MESH,
        )

    def row_copy(chunk):
        return pltpu.make_async_remote_copy(
            src_ref=resid_out.at[chunk],
            dst_ref=resid.at[chunk, pl.ds(td * rows, td * HALO_ROWS)],
            send_sem=row_send.at[chunk],
            recv_sem=row_recv.at[chunk],
            device_id={"rows": 1 - core},
            device_id_type=MESH,
        )

    def peak_copy(source, target):
        return pltpu.make_async_remote_copy(
            src_ref=peak_out,
            dst_ref=peak_all.at[source],
            send_sem=peak_send.at[target],
            recv_sem=peak_recv.at[source],
            device_id={"tm": target},
            device_id_type=MESH,
        )

    barrier = pltpu.get_barrier_semaphore()

    def greet(step, carry):
        pl.semaphore_signal(barrier, inc=1, device_id={"tm": peer(step)}, device_id_type=MESH)
        return carry

    lax.fori_loop(1, n, greet, 0)
    pl.semaphore_signal(barrier, inc=1, device_id={"rows": 1 - core}, device_id_type=MESH)
    pl.semaphore_wait(barrier, n)

    def send_first(step, carry):
        meta_copy(me, peer(step)).start()
        return carry

    lax.fori_loop(1, n, send_first, 0)

    def send_pixels(step, carry):
        x_copy(me, peer(step)).start()
        return carry

    lax.fori_loop(1, n, send_pixels, 0)

    side = 2 * RADIUS
    lane_in = lax.broadcasted_iota(jnp.int32, (LANES, 2 * LANES), 0)
    lane_out = lax.broadcasted_iota(jnp.int32, (LANES, 2 * LANES), 1)
    packed = jnp.zeros((n * rows, 2 * LANES), f32)
    for j in range(td):
        tiles = jnp.concatenate(
            [x_ref[j, :, d * LANES : (d + 1) * LANES] for d in range(n)], axis=0
        )
        to_right = (lane_in >= LANES - RADIUS) & (
            lane_out == lane_in - (LANES - RADIUS) + side * j
        )
        to_left = (lane_in < RADIUS) & (lane_out == LANES + lane_in + RADIUS + side * j)
        packed = packed + jnp.dot(
            tiles, (to_right | to_left).astype(f32).astype(bf16), preferred_element_type=f32
        )
    for d in range(n):
        tile = jnp.zeros((rows, LANES), f32)
        if d > 0:
            tile = tile + packed[(d - 1) * rows : d * rows, :LANES]
        if d < n - 1:
            tile = tile + packed[(d + 1) * rows : (d + 2) * rows, LANES:]
        halo_out[d] = tile.astype(bf16)

    def send_halo(step, carry):
        halo_copy(me, peer(step)).start()
        return carry

    lax.fori_loop(1, n, send_halo, 0)
    meta_all[me] = meta_ref[...]
    halo_all[me] = halo_out[me]
    x_all[me] = x_ref[:, :, lanes_of(me)]

    spread_in = lax.broadcasted_iota(jnp.int32, spread.shape, 0)
    spread_out = lax.broadcasted_iota(jnp.int32, spread.shape, 1)
    spread[...] = (
        (spread_out % LANES < side) & (spread_in == side * (spread_out // LANES) + spread_out % LANES)
    ).astype(f32).astype(bf16)
    lane = lax.broadcasted_iota(jnp.int32, (2 * LANES, LANES), 0)
    column = lax.broadcasted_iota(jnp.int32, (2 * LANES, LANES), 1)
    source_col = jnp.where(
        lane < LANES,
        lane,
        jnp.where(
            lane < LANES + RADIUS,
            lane - LANES - RADIUS,
            jnp.where(lane < LANES + side, lane - RADIUS, 4 * LANES),
        ),
    )
    column_offset = (source_col - column).astype(f32)
    for s in range(WIDTHS):
        col_tab[:, s * LANES : (s + 1) * LANES] = tap_values(column_offset, s + 1).astype(bf16)
    out_row = lax.broadcasted_iota(jnp.int32, (rows, 2 * LANES), 0)
    lane = lax.broadcasted_iota(jnp.int32, (rows, 2 * LANES), 1)
    own = lane < td * rows
    beside = lane - td * rows
    time_of = jnp.where(own, lane // rows, beside // HALO_ROWS)
    source_row = jnp.where(own, lane % rows, beside % HALO_ROWS + jnp.where(core == 0, rows, -HALO_ROWS))
    row_offset = (source_row - out_row).astype(f32)
    for s in range(WIDTHS):
        values = tap_values(row_offset, s + 1).astype(bf16).astype(f32)
        for j in range(td):
            row_tab[s, j] = jnp.where(time_of == j, values, 0.0)
    masked[0:HISTORY_FRAMES] = jnp.zeros((HISTORY_FRAMES,) + masked.shape[1:], f32)

    def wait_meta(step, carry):
        meta_copy(peer(step), me).wait_recv()
        return carry

    lax.fori_loop(1, n, wait_meta, 0)
    meta = meta_all[...].reshape(total, LANES).astype(bf16)
    entry = lax.broadcasted_iota(jnp.int32, (LANES, 2 * LANES), 0)
    lane = lax.broadcasted_iota(jnp.int32, (LANES, 2 * LANES), 1)
    tile_of = jnp.where(
        lane < LANES,
        me,
        jnp.where(lane < LANES + RADIUS, me - 1, jnp.where(lane < LANES + side, me + 1, -1)),
    )
    inside = (tile_of >= 0) & (tile_of < n)
    target = lax.broadcasted_iota(jnp.int32, (total, total), 0)
    source = lax.broadcasted_iota(jnp.int32, (total, total), 1)
    band = ((target - source >= 1) & (target - source <= HISTORY_FRAMES)).astype(f32).astype(bf16)
    for rt in range(2):
        pick = (inside & (entry == rt * n + tile_of)).astype(f32).astype(bf16)
        keep = jnp.dot(meta, pick, preferred_element_type=f32)
        counts = jnp.dot(band, keep.astype(bf16), preferred_element_type=f32)
        keep_rows[rt] = keep
        scale_rows[rt] = keep / jnp.maximum(counts, 1.0)
    for f in range(2):
        pick = (entry == 2 * n + f).astype(f32).astype(bf16)
        width_rows[f] = jnp.dot(meta, pick, preferred_element_type=f32)

    def weight_step(c, carry):
        first = pl.multiple_of(c * td, td)
        width = [width_rows[f, pl.ds(first, td), :] for f in range(2)]
        for j in range(td):
            for f in range(2):
                at = (2 * j + f) * rows
                chosen = jnp.broadcast_to(width[f][j : j + 1], (rows, 2 * LANES))
                row_w[c, at : at + rows, :] = pick_width(
                    chosen, [row_tab[s, j] for s in range(WIDTHS)]
                ).astype(bf16)
        return carry

    lax.fori_loop(0, n, weight_step, 0)

    def residual_step(c, window):
        @pl.when(c != me)
        def _():
            x_copy(c, me).wait_recv()
            halo_copy(c, me).wait_recv()

        first = pl.multiple_of(c * td, td)
        halo = jnp.dot(halo_all[c], spread[...], preferred_element_type=f32)
        keep = [keep_rows[rt, pl.ds(first, td), :] for rt in range(2)]
        scale = [scale_rows[rt, pl.ds(first, td), :] for rt in range(2)]
        window = list(window)
        pending = None
        for j in range(td):
            pixels = jnp.concatenate(
                [x_all[c, j].astype(f32), halo[:, j * LANES : (j + 1) * LANES]], axis=1
            )
            old = masked[first + j]
            values, residuals = [], []
            for rt in range(2):
                part = slice(rt * TILE_R, (rt + 1) * TILE_R)
                value = pixels[part] * keep[rt][j : j + 1]
                residuals.append(value - window[rt] * scale[rt][j : j + 1])
                window[rt] = window[rt] + (value - old[part])
                values.append(value)
            masked[first + j + HISTORY_FRAMES] = jnp.concatenate(values, axis=0)
            resid[c, j * rows : (j + 1) * rows, :] = jnp.concatenate(residuals, axis=0).astype(bf16)
            edge = jnp.where(core == 0, residuals[1], residuals[0])
            if j % 2 == 0:
                pending = edge
            else:
                at = (j // 2) * 2 * HALO_ROWS
                resid_out[c, at : at + 2 * HALO_ROWS, :] = jnp.concatenate(
                    [pending, edge], axis=0
                ).astype(bf16)
        row_copy(c).start()
        return tuple(window)

    blank = jnp.zeros((TILE_R, 2 * LANES), f32)
    lax.fori_loop(0, n, residual_step, (blank, blank))

    def filter_step(g, totals):
        excess, peak = list(totals[:2]), list(totals[2:])
        row_results, width = [], []
        for part in range(group):
            c = g * group + part
            row_copy(c).wait_recv()
            first = pl.multiple_of(c * td, td)
            width.append([width_rows[f, pl.ds(first, td), :] for f in range(2)])
            row_results.append(
                jnp.dot(
                    row_w[c, :, : td * (rows + HALO_ROWS)], resid[c], preferred_element_type=f32
                ).astype(bf16)
            )
        trial = jnp.dot(
            jnp.concatenate(row_results, axis=0), col_tab[...], preferred_element_type=f32
        )
        for part in range(group):
            for j in range(td):
                for f in range(2):
                    at = ((part * td + j) * 2 + f) * rows
                    chosen = jnp.broadcast_to(width[part][f][j : j + 1, :LANES], (rows, LANES))
                    filtered = pick_width(
                        chosen,
                        [
                            trial[at : at + rows, s * LANES : (s + 1) * LANES]
                            for s in range(WIDTHS)
                        ],
                    )
                    excess[f] = excess[f] + jnp.maximum(filtered - threshold, 0.0)
                    peak[f] = jnp.maximum(peak[f], filtered)
        return tuple(excess) + tuple(peak)

    group = 4 if n % 4 == 0 else 1
    zero = jnp.zeros((rows, LANES), f32)
    low = jnp.full((rows, LANES), -1e30, f32)
    results = lax.fori_loop(0, n // group, filter_step, (zero, zero, low, low))
    for f in range(2):
        peak_out[f] = results[2 + f].astype(bf16)

    def send_peak(step, carry):
        peak_copy(me, peer(step)).start()
        return carry

    lax.fori_loop(1, n, send_peak, 0)
    peak_all[me] = peak_out[...]
    for f in range(2):
        exc_ref[f] = results[f] * (1.0 / total)

    def finish_sends(step, carry):
        target = peer(step)
        x_copy(me, target).wait_send()
        meta_copy(me, target).wait_send()
        halo_copy(me, target).wait_send()
        return carry

    lax.fori_loop(1, n, finish_sends, 0)

    def finish_rows(c, carry):
        row_copy(c).wait_send()
        return carry

    lax.fori_loop(0, n, finish_rows, 0)

    def finish_peaks(step, carry):
        source = peer(step)
        peak_copy(source, me).wait_recv()
        peak_copy(me, source).wait_send()
        return carry

    lax.fori_loop(1, n, finish_peaks, 0)
    for d in range(n):
        peak_ref[:, :, d * LANES : (d + 1) * LANES] = peak_all[d].astype(f32)


def fused_body(n, snapshots, tile_masks, widths):
    td, rows, cols = snapshots.shape
    total = n * td
    filters = widths.shape[1]
    flat = tile_masks.reshape(td, -1)
    meta = jnp.concatenate([flat, widths], axis=1).astype(jnp.float32)
    meta = jnp.pad(meta, ((0, 0), (0, LANES - meta.shape[1])))
    f32, bf16 = jnp.float32, jnp.bfloat16
    depth = td * (rows + HALO_ROWS)
    dma = pltpu.SemaphoreType.DMA((n,))
    return pl.pallas_call(
        functools.partial(search_kernel, n),
        out_shape=(
            jax.ShapeDtypeStruct((filters, rows, LANES), f32),
            jax.ShapeDtypeStruct((filters, rows, cols), f32),
        ),
        in_specs=[pl.BlockSpec(memory_space=pltpu.VMEM)] * 2,
        out_specs=(pl.BlockSpec(memory_space=pltpu.VMEM),) * 2,
        scratch_shapes=[
            pltpu.VMEM((n, td, rows, LANES), bf16),
            pltpu.VMEM((n, rows, LANES), bf16),
            pltpu.VMEM((n, rows, LANES), bf16),
            pltpu.VMEM((n, td, LANES), f32),
            pltpu.VMEM((2, total, 2 * LANES), f32),
            pltpu.VMEM((2, total, 2 * LANES), f32),
            pltpu.VMEM((filters, total, 2 * LANES), f32),
            pltpu.VMEM((total + HISTORY_FRAMES, rows, 2 * LANES), f32),
            pltpu.VMEM((n, depth, 2 * LANES), bf16),
            pltpu.VMEM((n, td * HALO_ROWS, 2 * LANES), bf16),
            pltpu.VMEM((n, td * filters * rows, 2 * LANES), bf16),
            pltpu.VMEM((WIDTHS, td, rows, 2 * LANES), f32),
            pltpu.VMEM((2 * LANES, WIDTHS * LANES), bf16),
            pltpu.VMEM((LANES, td * LANES), bf16),
            pltpu.VMEM((filters, rows, LANES), bf16),
            pltpu.VMEM((n, filters, rows, LANES), bf16),
        ]
        + [dma] * 10,
        compiler_params=pltpu.CompilerParams(
            collective_id=0, has_side_effects=True, vmem_limit_bytes=40 * 2**20
        ),
    )(snapshots, meta)


def solution(mesh):
    count = mesh.shape["tm"]

    def per_device(snapshots, tile_masks, widths):
        td, rows, cols = snapshots.shape
        fits = (
            mesh.shape["rows"] == 2
            and (td, rows, widths.shape[1]) == (8, 2 * TILE_R, 2)
            and cols == count * LANES
            and 2 * count + 2 <= LANES
        )
        if fits:
            return fused_body(count, snapshots, tile_masks, widths)
        return body(snapshots, tile_masks, widths)

    return jax.shard_map(
        per_device,
        mesh=mesh,
        in_specs=(P("tm", "rows", None), P("tm", "rows", None), P("tm", None)),
        out_specs=(P(None, "rows", "tm"), P(None, "rows", None)),
        check_vma=False,
    )
```

```python
import functools
import math

import jax
import jax.numpy as jnp
from jax import lax
from jax.experimental import pallas as pl
from jax.experimental.pallas import tpu as pltpu
from jax.sharding import PartitionSpec as P

HISTORY_FRAMES = 64
RADIUS = 8
TILE_R = 8
TILE_C = 128


threshold = 0.5


def padded(value, sides, width):
    for axis, dim in sides:
        count, length = (lax.axis_size(axis), value.shape[dim])
        up = [(i, (i + 1) % count) for i in range(count - 1)]
        down = [(j, i) for i, j in up]
        last = lax.slice_in_dim(value, length - width, length, axis=dim)
        first = lax.slice_in_dim(value, 0, width, axis=dim)
        before = lax.ppermute(last, axis, up)
        after = lax.ppermute(first, axis, down)
        value = jnp.concatenate([before, value, after], axis=dim)
    return value


def filter_taps(widths):
    sigma_val = widths.astype(jnp.float32)[..., None]
    offsets = jnp.arange(-RADIUS, RADIUS + 1).astype(jnp.float32)
    weights = jnp.exp(-(offsets * offsets) / (2.0 * sigma_val * sigma_val))
    return (weights / jnp.sqrt(jnp.sum(weights * weights, axis=-1, keepdims=True))).astype(
        jnp.bfloat16
    )


def history_band(local_times, back_step):
    target = jnp.arange(local_times)[:, None]
    source = jnp.arange(local_times)[None, :]
    distance = back_step * local_times + target - source
    return ((distance >= 1) & (distance <= HISTORY_FRAMES)).astype(jnp.bfloat16)


def tap_onehot(target_count):
    taps_count = 2 * RADIUS + 1
    source = jnp.arange(target_count + 2 * RADIUS)[:, None, None]
    target = jnp.arange(target_count)[None, :, None]
    return (source - target == jnp.arange(taps_count)[None, None, :]).astype(jnp.float32)


def column_residual(snapshots, tile_masks, widths):
    moved = lax.all_to_all(snapshots, "tm", split_axis=2, concat_axis=0, tiled=True)
    all_masks, all_widths = (
        lax.all_gather(tile_masks, "tm", axis=0, tiled=True),
        lax.all_gather(widths, "tm", axis=0, tiled=True),
    )
    total_times, local_rows, own_cols = moved.shape
    patch_rows = all_masks.shape[1]
    first_col = lax.axis_index("tm") * own_cols
    tile_of = (first_col + jnp.arange(own_cols)) // TILE_C
    pick = (jnp.arange(all_masks.shape[2])[:, None] == tile_of[None, :]).astype(jnp.float32)
    keep_tiles = jnp.einsum("trk,kc->trc", all_masks.astype(jnp.float32), pick)
    keep_pixels = jnp.broadcast_to(
        keep_tiles[:, :, None, :], (total_times, patch_rows, TILE_R, own_cols)
    ).reshape(total_times, local_rows, own_cols)
    pixels = local_rows * own_cols
    keep_flat = keep_pixels.astype(jnp.bfloat16).reshape(total_times, pixels)
    masked = moved.reshape(total_times, pixels) * keep_flat
    block_count = total_times // HISTORY_FRAMES
    own_band = history_band(HISTORY_FRAMES, 0)
    back_band = history_band(HISTORY_FRAMES, 1)
    empty_block = jnp.zeros((1, HISTORY_FRAMES, pixels), jnp.bfloat16)
    value_blocks = masked.reshape(block_count, HISTORY_FRAMES, pixels)
    keep_blocks = keep_flat.reshape(block_count, HISTORY_FRAMES, pixels)
    value_prior = jnp.concatenate([empty_block, value_blocks[:-1]], axis=0)
    keep_prior = jnp.concatenate([empty_block, keep_blocks[:-1]], axis=0)
    window = jnp.einsum("js,bsp->bjp", own_band, value_blocks, preferred_element_type=jnp.float32)
    window = window + jnp.einsum(
        "js,bsp->bjp", back_band, value_prior, preferred_element_type=jnp.float32
    )
    counts = jnp.einsum("js,bsp->bjp", own_band, keep_blocks, preferred_element_type=jnp.float32)
    counts = counts + jnp.einsum(
        "js,bsp->bjp", back_band, keep_prior, preferred_element_type=jnp.float32
    )
    mean_img = (window / jnp.maximum(counts, 1.0)).reshape(total_times, local_rows, own_cols)
    residual = (keep_pixels * (moved.astype(jnp.float32) - mean_img)).astype(jnp.bfloat16)
    return (residual, filter_taps(all_widths).astype(jnp.float32))


def body(snapshots, tile_masks, widths):
    residual, kernel = column_residual(snapshots, tile_masks, widths)
    local_times, local_rows, column_count = residual.shape
    padded_rows = padded(residual, (("rows", 1),), RADIUS)
    row_onehot = tap_onehot(local_rows)
    row_results = []
    for filter_index in range(widths.shape[1]):
        row_weights = jnp.einsum(
            "jik,tk->tij", row_onehot, kernel[:, filter_index], precision=lax.Precision.HIGHEST
        ).astype(jnp.bfloat16)
        row_results.append(
            jnp.einsum(
                "tij,tjc->tic", row_weights, padded_rows, preferred_element_type=jnp.float32
            ).astype(jnp.bfloat16)
        )
    stacked_rows = jnp.stack(row_results)
    padded_cols = padded(stacked_rows, (("tm", 3),), RADIUS)
    column_onehot = tap_onehot(column_count)
    excess_terms = []
    peak_terms = []
    for filter_index in range(widths.shape[1]):
        column_weights = jnp.einsum(
            "jck,tk->tjc", column_onehot, kernel[:, filter_index], precision=lax.Precision.HIGHEST
        ).astype(jnp.bfloat16)
        filtered = jnp.einsum(
            "trj,tjc->trc",
            padded_cols[filter_index],
            column_weights,
            preferred_element_type=jnp.float32,
        )
        excess_terms.append(jnp.sum(jnp.maximum(filtered - threshold, 0.0), axis=0))
        peak_terms.append(jnp.max(filtered, axis=0))
    excess_map = jnp.stack(excess_terms) / local_times
    peak_map = lax.all_gather(jnp.stack(peak_terms), "tm", axis=2, tiled=True)
    return (excess_map, peak_map)


MESH = pl.DeviceIdType.MESH
WIDTHS = 4
LANES = 128
HALO_ROWS = 8


def tap_values(offset, width):
    norm = math.sqrt(sum(math.exp(-(k * k) / (width * width)) for k in range(-RADIUS, RADIUS + 1)))
    value = jnp.exp(offset * offset * (-1.0 / (2.0 * width * width))) / norm
    return jnp.where(jnp.abs(offset) <= RADIUS, value, 0.0)


def pick_width(width, options):
    first, second, third, fourth = options
    return jnp.where(
        width == 1.0,
        first,
        jnp.where(width == 2.0, second, jnp.where(width == 3.0, third, fourth)),
    )


def search_kernel(
    n,
    x_ref,
    meta_ref,
    exc_ref,
    peak_ref,
    x_all,
    halo_out,
    halo_all,
    meta_all,
    keep_rows,
    scale_rows,
    width_rows,
    masked,
    resid,
    resid_out,
    row_w,
    row_tab,
    col_tab,
    spread,
    peak_out,
    peak_all,
    x_send,
    x_recv,
    meta_send,
    meta_recv,
    halo_send,
    halo_recv,
    row_send,
    row_recv,
    peak_send,
    peak_recv,
):
    me, core = lax.axis_index("tm"), lax.axis_index("rows")
    td = x_ref.shape[0]
    rows = x_ref.shape[1]
    total = n * td
    f32, bf16 = jnp.float32, jnp.bfloat16

    def peer(step):
        return lax.rem(me + n - step, n)

    def lanes_of(band):
        return pl.ds(pl.multiple_of(band * LANES, LANES), LANES)

    def x_copy(source, target):
        return pltpu.make_async_remote_copy(
            src_ref=x_ref.at[:, :, lanes_of(target)],
            dst_ref=x_all.at[source],
            send_sem=x_send.at[target],
            recv_sem=x_recv.at[source],
            device_id={"tm": target},
            device_id_type=MESH,
        )

    def meta_copy(source, target):
        return pltpu.make_async_remote_copy(
            src_ref=meta_ref,
            dst_ref=meta_all.at[source],
            send_sem=meta_send.at[target],
            recv_sem=meta_recv.at[source],
            device_id={"tm": target},
            device_id_type=MESH,
        )

    def halo_copy(source, target):
        return pltpu.make_async_remote_copy(
            src_ref=halo_out.at[target],
            dst_ref=halo_all.at[source],
            send_sem=halo_send.at[target],
            recv_sem=halo_recv.at[source],
            device_id={"tm": target},
            device_id_type=MESH,
        )

    def row_copy(chunk):
        return pltpu.make_async_remote_copy(
            src_ref=resid_out.at[chunk],
            dst_ref=resid.at[chunk, pl.ds(td * rows, td * HALO_ROWS)],
            send_sem=row_send.at[chunk],
            recv_sem=row_recv.at[chunk],
            device_id={"rows": 1 - core},
            device_id_type=MESH,
        )

    def peak_copy(source, target):
        return pltpu.make_async_remote_copy(
            src_ref=peak_out,
            dst_ref=peak_all.at[source],
            send_sem=peak_send.at[target],
            recv_sem=peak_recv.at[source],
            device_id={"tm": target},
            device_id_type=MESH,
        )

    barrier = pltpu.get_barrier_semaphore()

    def greet(step, carry):
        pl.semaphore_signal(barrier, inc=1, device_id={"tm": peer(step)}, device_id_type=MESH)
        return carry

    lax.fori_loop(1, n, greet, 0)
    pl.semaphore_signal(barrier, inc=1, device_id={"rows": 1 - core}, device_id_type=MESH)
    pl.semaphore_wait(barrier, n)

    def send_first(step, carry):
        meta_copy(me, peer(step)).start()
        return carry

    lax.fori_loop(1, n, send_first, 0)

    def send_pixels(step, carry):
        x_copy(me, peer(step)).start()
        return carry

    lax.fori_loop(1, n, send_pixels, 0)

    side = 2 * RADIUS
    lane_in = lax.broadcasted_iota(jnp.int32, (LANES, 2 * LANES), 0)
    lane_out = lax.broadcasted_iota(jnp.int32, (LANES, 2 * LANES), 1)
    packed = jnp.zeros((n * rows, 2 * LANES), f32)
    for j in range(td):
        tiles = jnp.concatenate(
            [x_ref[j, :, d * LANES : (d + 1) * LANES] for d in range(n)], axis=0
        )
        to_right = (lane_in >= LANES - RADIUS) & (
            lane_out == lane_in - (LANES - RADIUS) + side * j
        )
        to_left = (lane_in < RADIUS) & (lane_out == LANES + lane_in + RADIUS + side * j)
        packed = packed + jnp.dot(
            tiles, (to_right | to_left).astype(f32).astype(bf16), preferred_element_type=f32
        )
    for d in range(n):
        tile = jnp.zeros((rows, LANES), f32)
        if d > 0:
            tile = tile + packed[(d - 1) * rows : d * rows, :LANES]
        if d < n - 1:
            tile = tile + packed[(d + 1) * rows : (d + 2) * rows, LANES:]
        halo_out[d] = tile.astype(bf16)

    def send_halo(step, carry):
        halo_copy(me, peer(step)).start()
        return carry

    lax.fori_loop(1, n, send_halo, 0)
    meta_all[me] = meta_ref[...]
    halo_all[me] = halo_out[me]
    x_all[me] = x_ref[:, :, lanes_of(me)]

    spread_in = lax.broadcasted_iota(jnp.int32, spread.shape, 0)
    spread_out = lax.broadcasted_iota(jnp.int32, spread.shape, 1)
    spread[...] = (
        (spread_out % LANES < side) & (spread_in == side * (spread_out // LANES) + spread_out % LANES)
    ).astype(f32).astype(bf16)
    lane = lax.broadcasted_iota(jnp.int32, (2 * LANES, LANES), 0)
    column = lax.broadcasted_iota(jnp.int32, (2 * LANES, LANES), 1)
    source_col = jnp.where(
        lane < LANES,
        lane,
        jnp.where(
            lane < LANES + RADIUS,
            lane - LANES - RADIUS,
            jnp.where(lane < LANES + side, lane - RADIUS, 4 * LANES),
        ),
    )
    column_offset = (source_col - column).astype(f32)
    for s in range(WIDTHS):
        col_tab[:, s * LANES : (s + 1) * LANES] = tap_values(column_offset, s + 1).astype(bf16)
    out_row = lax.broadcasted_iota(jnp.int32, (rows, 2 * LANES), 0)
    lane = lax.broadcasted_iota(jnp.int32, (rows, 2 * LANES), 1)
    own = lane < td * rows
    beside = lane - td * rows
    time_of = jnp.where(own, lane // rows, beside // HALO_ROWS)
    source_row = jnp.where(own, lane % rows, beside % HALO_ROWS + jnp.where(core == 0, rows, -HALO_ROWS))
    row_offset = (source_row - out_row).astype(f32)
    for s in range(WIDTHS):
        values = tap_values(row_offset, s + 1).astype(bf16).astype(f32)
        for j in range(td):
            row_tab[s, j] = jnp.where(time_of == j, values, 0.0)
    masked[0:HISTORY_FRAMES] = jnp.zeros((HISTORY_FRAMES,) + masked.shape[1:], f32)

    def wait_meta(step, carry):
        meta_copy(peer(step), me).wait_recv()
        return carry

    lax.fori_loop(1, n, wait_meta, 0)
    meta = meta_all[...].reshape(total, LANES).astype(bf16)
    entry = lax.broadcasted_iota(jnp.int32, (LANES, 2 * LANES), 0)
    lane = lax.broadcasted_iota(jnp.int32, (LANES, 2 * LANES), 1)
    tile_of = jnp.where(
        lane < LANES,
        me,
        jnp.where(lane < LANES + RADIUS, me - 1, jnp.where(lane < LANES + side, me + 1, -1)),
    )
    inside = (tile_of >= 0) & (tile_of < n)
    target = lax.broadcasted_iota(jnp.int32, (total, total), 0)
    source = lax.broadcasted_iota(jnp.int32, (total, total), 1)
    band = ((target - source >= 1) & (target - source <= HISTORY_FRAMES)).astype(f32).astype(bf16)
    for rt in range(2):
        pick = (inside & (entry == rt * n + tile_of)).astype(f32).astype(bf16)
        keep = jnp.dot(meta, pick, preferred_element_type=f32)
        counts = jnp.dot(band, keep.astype(bf16), preferred_element_type=f32)
        keep_rows[rt] = keep
        scale_rows[rt] = keep / jnp.maximum(counts, 1.0)
    for f in range(2):
        pick = (entry == 2 * n + f).astype(f32).astype(bf16)
        width_rows[f] = jnp.dot(meta, pick, preferred_element_type=f32)

    def weight_step(c, carry):
        first = pl.multiple_of(c * td, td)
        width = [width_rows[f, pl.ds(first, td), :] for f in range(2)]
        for j in range(td):
            for f in range(2):
                at = (2 * j + f) * rows
                chosen = jnp.broadcast_to(width[f][j : j + 1], (rows, 2 * LANES))
                row_w[c, at : at + rows, :] = pick_width(
                    chosen, [row_tab[s, j] for s in range(WIDTHS)]
                ).astype(bf16)
        return carry

    lax.fori_loop(0, n, weight_step, 0)

    def residual_step(c, window):
        @pl.when(c != me)
        def _():
            x_copy(c, me).wait_recv()
            halo_copy(c, me).wait_recv()

        first = pl.multiple_of(c * td, td)
        halo = jnp.dot(halo_all[c], spread[...], preferred_element_type=f32)
        keep = [keep_rows[rt, pl.ds(first, td), :] for rt in range(2)]
        scale = [scale_rows[rt, pl.ds(first, td), :] for rt in range(2)]
        window = list(window)
        pending = None
        for j in range(td):
            pixels = jnp.concatenate(
                [x_all[c, j].astype(f32), halo[:, j * LANES : (j + 1) * LANES]], axis=1
            )
            old = masked[first + j]
            values, residuals = [], []
            for rt in range(2):
                part = slice(rt * TILE_R, (rt + 1) * TILE_R)
                value = pixels[part] * keep[rt][j : j + 1]
                residuals.append(value - window[rt] * scale[rt][j : j + 1])
                window[rt] = window[rt] + (value - old[part])
                values.append(value)
            masked[first + j + HISTORY_FRAMES] = jnp.concatenate(values, axis=0)
            resid[c, j * rows : (j + 1) * rows, :] = jnp.concatenate(residuals, axis=0).astype(bf16)
            edge = jnp.where(core == 0, residuals[1], residuals[0])
            if j % 2 == 0:
                pending = edge
            else:
                at = (j // 2) * 2 * HALO_ROWS
                resid_out[c, at : at + 2 * HALO_ROWS, :] = jnp.concatenate(
                    [pending, edge], axis=0
                ).astype(bf16)
        row_copy(c).start()
        return tuple(window)

    blank = jnp.zeros((TILE_R, 2 * LANES), f32)

    def filter_step(g, totals):
        excess, peak = list(totals[:2]), list(totals[2:])
        row_results, width = [], []
        for part in range(group):
            c = g * group + part
            row_copy(c).wait_recv()
            first = pl.multiple_of(c * td, td)
            width.append([width_rows[f, pl.ds(first, td), :] for f in range(2)])
            row_results.append(
                jnp.dot(
                    row_w[c, :, : td * (rows + HALO_ROWS)], resid[c], preferred_element_type=f32
                ).astype(bf16)
            )
        trial = jnp.dot(
            jnp.concatenate(row_results, axis=0), col_tab[...], preferred_element_type=f32
        )
        for part in range(group):
            for j in range(td):
                for f in range(2):
                    at = ((part * td + j) * 2 + f) * rows
                    chosen = jnp.broadcast_to(width[part][f][j : j + 1, :LANES], (rows, LANES))
                    filtered = pick_width(
                        chosen,
                        [
                            trial[at : at + rows, s * LANES : (s + 1) * LANES]
                            for s in range(WIDTHS)
                        ],
                    )
                    excess[f] = excess[f] + jnp.maximum(filtered - threshold, 0.0)
                    peak[f] = jnp.maximum(peak[f], filtered)
        return tuple(excess) + tuple(peak)

    group = 4 if n % 4 == 0 else 1
    zero = jnp.zeros((rows, LANES), f32)
    low = jnp.full((rows, LANES), -1e30, f32)

    def residual_group(g, window):
        return lax.fori_loop(
            0, group, lambda part, carry: residual_step(g * group + part, carry), window
        )

    def both(g, carry):
        return residual_group(g, carry[:2]) + filter_step(g - 1, carry[2:])

    carry = residual_group(0, (blank, blank)) + (zero, zero, low, low)
    carry = lax.fori_loop(1, n // group, both, carry)
    results = filter_step(n // group - 1, carry[2:])
    for f in range(2):
        peak_out[f] = results[2 + f].astype(bf16)

    def send_peak(step, carry):
        peak_copy(me, peer(step)).start()
        return carry

    lax.fori_loop(1, n, send_peak, 0)
    peak_all[me] = peak_out[...]
    for f in range(2):
        exc_ref[f] = results[f] * (1.0 / total)

    def finish_sends(step, carry):
        target = peer(step)
        x_copy(me, target).wait_send()
        meta_copy(me, target).wait_send()
        halo_copy(me, target).wait_send()
        return carry

    lax.fori_loop(1, n, finish_sends, 0)

    def finish_rows(c, carry):
        row_copy(c).wait_send()
        return carry

    lax.fori_loop(0, n, finish_rows, 0)

    def finish_peaks(step, carry):
        source = peer(step)
        peak_copy(source, me).wait_recv()
        peak_copy(me, source).wait_send()
        return carry

    lax.fori_loop(1, n, finish_peaks, 0)
    for d in range(n):
        peak_ref[:, :, d * LANES : (d + 1) * LANES] = peak_all[d].astype(f32)


def fused_body(n, snapshots, tile_masks, widths):
    td, rows, cols = snapshots.shape
    total = n * td
    filters = widths.shape[1]
    flat = tile_masks.reshape(td, -1)
    meta = jnp.concatenate([flat, widths], axis=1).astype(jnp.float32)
    meta = jnp.pad(meta, ((0, 0), (0, LANES - meta.shape[1])))
    f32, bf16 = jnp.float32, jnp.bfloat16
    depth = td * (rows + HALO_ROWS)
    dma = pltpu.SemaphoreType.DMA((n,))
    return pl.pallas_call(
        functools.partial(search_kernel, n),
        out_shape=(
            jax.ShapeDtypeStruct((filters, rows, LANES), f32),
            jax.ShapeDtypeStruct((filters, rows, cols), f32),
        ),
        in_specs=[pl.BlockSpec(memory_space=pltpu.VMEM)] * 2,
        out_specs=(pl.BlockSpec(memory_space=pltpu.VMEM),) * 2,
        scratch_shapes=[
            pltpu.VMEM((n, td, rows, LANES), bf16),
            pltpu.VMEM((n, rows, LANES), bf16),
            pltpu.VMEM((n, rows, LANES), bf16),
            pltpu.VMEM((n, td, LANES), f32),
            pltpu.VMEM((2, total, 2 * LANES), f32),
            pltpu.VMEM((2, total, 2 * LANES), f32),
            pltpu.VMEM((filters, total, 2 * LANES), f32),
            pltpu.VMEM((total + HISTORY_FRAMES, rows, 2 * LANES), f32),
            pltpu.VMEM((n, depth, 2 * LANES), bf16),
            pltpu.VMEM((n, td * HALO_ROWS, 2 * LANES), bf16),
            pltpu.VMEM((n, td * filters * rows, 2 * LANES), bf16),
            pltpu.VMEM((WIDTHS, td, rows, 2 * LANES), f32),
            pltpu.VMEM((2 * LANES, WIDTHS * LANES), bf16),
            pltpu.VMEM((LANES, td * LANES), bf16),
            pltpu.VMEM((filters, rows, LANES), bf16),
            pltpu.VMEM((n, filters, rows, LANES), bf16),
        ]
        + [dma] * 10,
        compiler_params=pltpu.CompilerParams(
            collective_id=0, has_side_effects=True, vmem_limit_bytes=40 * 2**20
        ),
    )(snapshots, meta)


def solution(mesh):
    count = mesh.shape["tm"]

    def per_device(snapshots, tile_masks, widths):
        td, rows, cols = snapshots.shape
        fits = (
            mesh.shape["rows"] == 2
            and (td, rows, widths.shape[1]) == (8, 2 * TILE_R, 2)
            and cols == count * LANES
            and 2 * count + 2 <= LANES
        )
        if fits:
            return fused_body(count, snapshots, tile_masks, widths)
        return body(snapshots, tile_masks, widths)

    return jax.shard_map(
        per_device,
        mesh=mesh,
        in_specs=(P("tm", "rows", None), P("tm", "rows", None), P("tm", None)),
        out_specs=(P(None, "rows", "tm"), P(None, "rows", None)),
        check_vma=False,
    )
```
